256 devices in a mesh: wide: 64 (over x, z_lo, y), slab: 4 (over z_hi, core).
Axes of the slice: x: 4, y: 4, z: 8 (z_hi: 2, z_lo: 4; z = z_hi * 4 + z_lo), core: 2. Of those that a mesh axis runs over, the one named last changes fastest.
Arguments:
- volume: bfloat16 [5, 8, 32768], P(None, 'slab', 'wide'), may hold values from -6 to 6
- back_proj: float32 [8, 32768], P('slab', 'wide'), may hold values from -6 to 6
- dual_state: bfloat16 [5, 8, 128, 1024], P(None, 'slab', 'wide'), may hold values from -6 to 6
- sinogram: bfloat16 [8, 128, 1024], P('slab', 'wide'), may hold values from -6 to 6
- offsets: int32 [64, 128], replicated, may hold values from 0 to 960
- primal_first: bfloat16 [3, 3, 3, 6, 32], replicated, may hold values from -0.5 to 0.5
- primal_second: bfloat16 [3, 3, 3, 32, 32], replicated, may hold values from -0.21875 to 0.21875
- primal_third: bfloat16 [3, 3, 3, 32, 5], replicated, may hold values from -0.21875 to 0.21875
- dual_first: bfloat16 [3, 3, 3, 7, 32], replicated, may hold values from -0.4375 to 0.4375
- dual_second: bfloat16 [3, 3, 3, 32, 32], replicated, may hold values from -0.21875 to 0.21875
- dual_third: bfloat16 [3, 3, 3, 32, 5], replicated, may hold values from -0.21875 to 0.21875
Outputs:
- new_volume: bfloat16 [5, 8, 32768], P(None, 'slab', 'wide')
- new_dual: bfloat16 [5, 8, 128, 1024], P(None, 'slab', 'wide')
- new_back: float32 [8, 32768], P('slab', 'wide')
The draws below stay inside these ranges and needn't reach their ends.
Inputs may be any that keep to these rules, and one draw needn't show every extreme that they name: offsets[t, a] is where tile t's window of 64 bins begins on the detector at angle a.
All inputs are finite; a program needn't handle non-finite values.
Results may differ from the reference program's by a relative error of at most 0.005.
Values may be sent and summed in bfloat16 or wider, within the bound.
No kernel may reach another device: no remote copies, remote signals or barrier semaphores. Data moves between devices by JAX's collectives and lax.ppermute only.
A program may use at most 64 MiB of HBM per device.

```python
import math
import jax
import jax.numpy as jnp
from jax import lax

C = 32
MEM = 5
NBINS = 1024
NY = 32
TX = 16
NX = 1024
NZ = 8
ANGLES = 128
N_WIDE = 64


def touch_ends(values, key, least, top_value):
    shape = values.shape
    index_at = [jax.random.randint(jax.random.fold_in(key, axis), (), 0, shape[axis]) for axis in range(len(shape))]
    values = values.at[tuple(index_at)].set(least)
    longest = shape.index(max(shape))
    index_at[longest] = (index_at[longest] + 1) % shape[longest]
    return values.at[tuple(index_at)].set(top_value)


def levels(rng, dims, cuts, low, top_value):
    level = 1.0
    for position, parts in cuts:
        draws = jax.random.uniform(jax.random.fold_in(jax.random.fold_in(rng, 6), position), (parts,), jnp.float32, low / len(cuts), top_value / len(cuts))
        level = level * jnp.repeat(jnp.exp(draws), dims[position] // parts).reshape((-1,) + (1,) * (len(dims) - 1 - position))
    return level


def bell_draw(stream_key, extent, scale, limit, split=(), held_as=jnp.bfloat16):
    level = levels(stream_key, extent, split, -0.22, 0.18) if split else 1.0
    entries = jax.random.normal(stream_key, extent, jnp.float32) * scale * level
    return jnp.minimum(jnp.maximum(entries, -limit), limit).astype(held_as)


def setup_inputs(seed: int = 0) -> dict:
    splits = jax.random.split(jax.random.key(seed), 12)
    volume = bell_draw(splits[0], (MEM, NZ, NX * NY), 1.0, 6.0, ((1, 4), (2, 64)))
    back_proj = bell_draw(splits[1], (NZ, NX * NY), 1.0, 6.0, ((0, 4), (1, 64)), jnp.float32)
    dual_state = bell_draw(splits[2], (MEM, NZ, ANGLES, NBINS), 1.0, 6.0, ((1, 4), (2, 64)))
    sinogram = bell_draw(splits[3], (NZ, ANGLES, NBINS), 1.0, 6.0, ((0, 4), (1, 64)))
    offsets = touch_ends(jax.random.randint(splits[4], (N_WIDE, ANGLES), 0, NBINS - NY - 2 * TX + 1), jax.random.fold_in(splits[4], 1), 0, NBINS - NY - 2 * TX).astype(jnp.int32)
    primal_first = bell_draw(splits[5], (3, 3, 3, MEM + 1, C), (27 * (MEM + 1)) ** -0.5, 0.5)
    primal_second = bell_draw(splits[6], (3, 3, 3, C, C), (27 * C) ** -0.5, 0.21875)
    primal_third = bell_draw(splits[7], (3, 3, 3, C, MEM), (27 * C) ** -0.5, 0.21875)
    dual_first = bell_draw(splits[8], (3, 3, 3, MEM + 2, C), (27 * (MEM + 2)) ** -0.5, 0.4375)
    dual_second = bell_draw(splits[9], (3, 3, 3, C, C), (27 * C) ** -0.5, 0.21875)
    dual_third = bell_draw(splits[10], (3, 3, 3, C, MEM), (27 * C) ** -0.5, 0.21875)
    return {"volume": volume, "back_proj": back_proj, "dual_state": dual_state, "sinogram": sinogram, "offsets": offsets, "primal_first": primal_first, "primal_second": primal_second, "primal_third": primal_third, "dual_first": dual_first, "dual_second": dual_second, "dual_third": dual_third}


def make_table(angle_ids, angle_total, rows_x, cols_y):
    window_bins = cols_y + 2 * rows_x
    angle_value = angle_ids.astype(jnp.float32) * (math.pi / angle_total)
    pixels = jnp.arange(rows_x * cols_y, dtype=jnp.int32)
    centre_x = (pixels // cols_y).astype(jnp.float32) - (rows_x - 1) / 2.0
    centre_y = (pixels % cols_y).astype(jnp.float32) - (cols_y - 1) / 2.0
    positions = centre_x[None, :] * jnp.cos(angle_value)[:, None] + centre_y[None, :] * jnp.sin(angle_value)[:, None] + window_bins / 2.0
    detector = jnp.arange(window_bins, dtype=jnp.int32).astype(jnp.float32)
    return jnp.maximum(0.0, 1.0 - jnp.abs(positions[:, :, None] - detector)).astype(jnp.bfloat16)

def convolve(field, weights):
    source = field.astype(jnp.float32)[None]
    kernel = weights.astype(jnp.float32)
    result = lax.conv_general_dilated(source, kernel, (1, 1, 1), ((1, 1), (1, 1), (1, 1)), dimension_numbers=('NCDHW', 'DHWIO', 'NCDHW'), precision=lax.Precision.HIGHEST)
    return result[0]

def reference(volume, back_proj, dual_state, sinogram, offsets, primal_first, primal_second, primal_third, dual_first, dual_second, dual_third):
    grid_view = volume.reshape(MEM, NZ, NX, NY)
    extra_channel = back_proj.astype(jnp.bfloat16).reshape(1, NZ, NX, NY)
    stacked = jnp.concatenate([grid_view, extra_channel], axis=0)
    hidden = jax.nn.relu(convolve(stacked, primal_first)).astype(jnp.bfloat16)
    hidden = jax.nn.relu(convolve(hidden, primal_second)).astype(jnp.bfloat16)
    new_volume = (grid_view.astype(jnp.float32) + convolve(hidden, primal_third)).astype(jnp.bfloat16).reshape(MEM, NZ, NX * NY)
    window_bins = NY + 2 * TX
    pixel_count = TX * NY
    table = make_table(jnp.arange(ANGLES, dtype=jnp.int32), ANGLES, TX, NY).astype(jnp.float32)
    leading = new_volume[0].reshape(NZ, N_WIDE, pixel_count).astype(jnp.float32)
    windows = jnp.einsum('ztp,apj->tazj', leading, table).astype(jnp.bfloat16)
    zero_index = jnp.zeros((), jnp.int32)

    def place_window(window_piece, start_bin):
        return lax.dynamic_update_slice(jnp.zeros((NZ, NBINS), jnp.float32), window_piece.astype(jnp.float32), (zero_index, start_bin))

    def place_tile(tile_id, running):
        spread = jax.vmap(place_window)(windows[tile_id], offsets[tile_id])
        return running + spread
    placed = lax.fori_loop(0, N_WIDE, place_tile, jnp.zeros((ANGLES, NZ, NBINS), jnp.float32))
    projected = (placed * (1.0 / math.sqrt(NY))).transpose(1, 0, 2).astype(jnp.bfloat16)
    dual_in = jnp.concatenate([dual_state, projected[None], sinogram[None]], axis=0)
    hidden = jax.nn.relu(convolve(dual_in, dual_first)).astype(jnp.bfloat16)
    hidden = jax.nn.relu(convolve(hidden, dual_second)).astype(jnp.bfloat16)
    new_dual = (dual_state.astype(jnp.float32) + convolve(hidden, dual_third)).astype(jnp.bfloat16)
    by_angle = new_dual[0].transpose(1, 0, 2)

    def cut_window(plane, start_bin):
        return lax.dynamic_slice(plane, (zero_index, start_bin), (NZ, window_bins))

    def back_tile(tile_id):
        pieces = jax.vmap(cut_window)(by_angle, offsets[tile_id])
        return jnp.einsum('azj,apj->zp', pieces.astype(jnp.float32), table)
    per_tile = lax.map(back_tile, jnp.arange(N_WIDE, dtype=jnp.int32))
    new_back = per_tile.transpose(1, 0, 2).reshape(NZ, NX * NY) * (1.0 / math.sqrt(ANGLES))
    return (new_volume, new_dual, new_back)
```

```python
import math

import jax
import jax.numpy as jnp
from jax import lax
from jax.experimental import pallas as pl
from jax.experimental.pallas import tpu as pltpu
from jax.sharding import PartitionSpec as P

NY = 32
TX = 16
BINS = NY + 2 * TX
HALO = 3
BF = jnp.bfloat16
F32 = jnp.float32
VMEM_BYTES = 48 * 1024 * 1024


def shifted(axis, delta, value):
    size = lax.axis_size(axis)
    return lax.ppermute(value, axis, [(i, i + delta) for i in range(size) if 0 <= i + delta < size])


def band(zo, zi_count):
    zi = jnp.arange(zi_count, dtype=jnp.int32)
    d = jnp.arange(3, dtype=jnp.int32)
    return ((zi[None, :, None] - zo[:, None, None] + 1) == d[None, None, :]).astype(BF)


def hidden_weights(w, nz):
    c, o = w.shape[3], w.shape[4]
    base = w.transpose(4, 1, 2, 0, 3).reshape(o, 9, 3 * c)
    width = nz * c
    wide = jnp.pad(base, ((0, 0), (0, 0), (width - c, width - 2 * c)))
    rows = [wide[:, :, (nz - zo) * c : (nz - zo) * c + width] for zo in range(nz)]
    return jnp.stack(rows).reshape(nz * o, 9 * width)


def table_kernel(angles, u_ref, u8_ref, t_ref, t8_ref):
    j = lax.broadcasted_iota(jnp.int32, (BINS, TX * NY), 0).astype(F32)

    def one(a, _):
        row = u_ref[pl.ds(a, 1), :]
        t_ref[pl.ds(pl.multiple_of(a * BINS, BINS), BINS), :] = jnp.maximum(0.0, 1.0 - jnp.abs(row - j)).astype(BF)
        return 0

    lax.fori_loop(0, angles, one, 0)
    for a in range(8):
        t8_ref[a * BINS : (a + 1) * BINS, :] = jnp.maximum(0.0, 1.0 - jnp.abs(u8_ref[a : a + 1, :] - j)).astype(BF)


def positions(angle_ids, angle_total):
    angle_value = angle_ids.astype(F32) * (math.pi / angle_total)
    pixels = jnp.arange(TX * NY, dtype=jnp.int32)
    centre_x = (pixels // NY).astype(F32) - (TX - 1) / 2.0
    centre_y = (pixels % NY).astype(F32) - (NY - 1) / 2.0
    return (
        centre_x[None, :] * jnp.cos(angle_value)[:, None]
        + centre_y[None, :] * jnp.sin(angle_value)[:, None]
        + BINS / 2.0
    )


def primal_kernel(nx, scal_ref, x_ref, w1_ref, w2_ref, w3_ref, own_ref, lead_ref, col1, col2):
    lanes = x_ref.shape[1]
    lane = lax.broadcasted_iota(jnp.int32, (1, lanes), 1)
    y = lane & (NY - 1)
    gx = (lane >> 5) - HALO + scal_ref[0] * TX
    inside = (gx >= 0) & (gx < nx)

    def fill(col, value):
        rows = value.shape[0]
        for dx in range(3):
            for dy in range(3):
                shift = NY * (dx - 1) + dy - 1
                moved = value if shift == 0 else pltpu.roll(value, (-shift) % lanes, 1)
                if dy == 0:
                    moved = jnp.where(y == 0, 0.0, moved)
                elif dy == 2:
                    moved = jnp.where(y == NY - 1, 0.0, moved)
                at = (dx * 3 + dy) * rows
                col[at : at + rows, :] = moved.astype(BF)

    x = x_ref[...].astype(F32)
    fill(col1, x)
    h = jnp.dot(w1_ref[...], col1[...], preferred_element_type=F32)
    h = jnp.where(inside, jnp.maximum(h, 0.0), 0.0)
    fill(col2, h)
    h = jnp.dot(w2_ref[...], col2[...], preferred_element_type=F32)
    h = jnp.where(inside, jnp.maximum(h, 0.0), 0.0).astype(BF)
    parts = jnp.dot(w3_ref[...], h, preferred_element_type=F32)
    rows = x.shape[0]
    total = x
    for dy in range(3):
        acc = jnp.zeros((rows, lanes), F32)
        for dx in range(3):
            at = (dx * 3 + dy) * rows
            part = parts[at : at + rows, :]
            if dx != 1:
                part = pltpu.roll(part, (-NY * (dx - 1)) % lanes, 1)
            acc = acc + part
        if dy == 0:
            acc = jnp.where(y == 0, 0.0, pltpu.roll(acc, 1, 1))
        elif dy == 2:
            acc = jnp.where(y == NY - 1, 0.0, pltpu.roll(acc, lanes - 1, 1))
        total = total + acc
    total = pltpu.roll(total, lanes - HALO * NY, 1)[:, : TX * NY]
    per = rows // 4
    lead_ref[...] = jnp.concatenate([total[i * per : i * per + 2] for i in range(4)], axis=0).astype(BF)
    own = jnp.zeros((per, TX * NY), F32)
    for i in range(4):
        own = jnp.where(scal_ref[1] == i, total[i * per : (i + 1) * per], own)
    own_ref[...] = own[: own_ref.shape[0]].astype(BF)


def dual_kernel(
    tiles, angles, scal_ref, off_ref, gv_ref, t8_ref, xk_ref, w1_ref, w2_ref, w3_ref, ds_ref,
    out_ref, piece_ref, win, pj, x1, h1, h2, parts, nd, pc,
):
    nb = x1.shape[2]
    blocks = nb // 128
    lane = lax.broadcasted_iota(jnp.int32, (8, 128), 1)
    big = lax.broadcasted_iota(jnp.int32, (1, nb), 1)
    first_angle = scal_ref[0] * 2 - HALO

    def before(v):
        return jnp.where(big == 0, 0.0, pltpu.roll(v, 1, 1))

    def after(v):
        return jnp.where(big == nb - 1, 0.0, pltpu.roll(v, nb - 1, 1))

    windows = lax.dot_general(
        gv_ref[...], t8_ref[...], (((1,), (1,)), ((), ())), preferred_element_type=F32
    )
    win[...] = windows.astype(BF).astype(F32)
    pj[...] = jnp.zeros(pj.shape, F32)

    def place(t, _):
        for a in range(8):
            off = off_ref[t, a]
            q = off >> 7
            r = off & 127
            v = win[pl.ds(pl.multiple_of(t * 8, 8), 8), (a // 2) * 128 : (a // 2) * 128 + 128]
            moved = pltpu.roll(v, (r + 64 * (a % 2)) & 127, 1)
            lo = jnp.where((lane >= r) & (lane < r + 64), moved, 0.0)
            hi = jnp.where(lane < r - 64, moved, 0.0)
            pj[a, q] += lo
            pj[a, q + 1] += hi
        return 0

    lax.fori_loop(0, tiles, place, 0)

    for a in range(8):
        valid = ((first_angle + a) >= 0) & ((first_angle + a) < angles)
        known = xk_ref[a].astype(F32)
        proj = jnp.concatenate([pj[a, b] for b in range(blocks)], axis=1) * (1.0 / math.sqrt(NY))
        proj = jnp.where(valid, proj, 0.0).astype(BF).astype(F32)
        x1[a] = jnp.concatenate(
            [before(known), known, after(known), before(proj), proj, after(proj), jnp.zeros((8, nb), F32)], axis=0
        ).astype(BF)

    k1 = x1.shape[1]
    for a in range(6):
        valid = ((first_angle + a + 1) >= 0) & ((first_angle + a + 1) < angles)
        h = jnp.dot(w1_ref[...], x1[a : a + 3].reshape(3 * k1, nb), preferred_element_type=F32)
        h = jnp.where(valid, jnp.maximum(h, 0.0), 0.0)
        rows = h.shape[0]
        h1[a, 0:rows] = before(h).astype(BF)
        h1[a, rows : 2 * rows] = h.astype(BF)
        h1[a, 2 * rows : 3 * rows] = after(h).astype(BF)

    k2 = h1.shape[1]
    for a in range(4):
        valid = ((first_angle + a + 2) >= 0) & ((first_angle + a + 2) < angles)
        h = jnp.dot(w2_ref[...], h1[a : a + 3].reshape(3 * k2, nb), preferred_element_type=F32)
        h2[a] = jnp.where(valid, jnp.maximum(h, 0.0), 0.0).astype(BF)
        parts[a] = jnp.dot(w3_ref[...], h2[a], preferred_element_type=F32)

    nd[...] = jnp.zeros(nd.shape, F32)
    for a in range(2):
        acc = []
        for db in range(3):
            acc.append(sum(parts[a + da, (da * 3 + db) * 16 : (da * 3 + db) * 16 + 16] for da in range(3)))
        result = before(acc[0]) + acc[1] + after(acc[2])
        result = (ds_ref[a].astype(F32) + result[:10]).astype(BF)
        out_ref[a] = result
        lead = result.astype(F32)[:2]
        lead = jnp.concatenate([lead] * 4, axis=0)
        for b in range(blocks):
            nd[a, b] = lead[:, b * 128 : (b + 1) * 128]

    sub = lax.broadcasted_iota(jnp.int32, (8, 128), 0) >> 1

    def cut(g, _):
        full = jnp.zeros((8, 128), F32)
        for i in range(4):
            got = []
            for a in range(2):
                off = off_ref[g * 4 + i, HALO + a]
                q = off >> 7
                r = off & 127
                v = jnp.where(lane >= r, nd[a, q], nd[a, q + 1])
                got.append(pltpu.roll(v, (64 * a + 128 - r) & 127, 1))
            full = jnp.where(sub == i, jnp.where(lane < 64, got[0], got[1]), full)
        pc[pl.ds(pl.multiple_of(g * 8, 8), 8), :] = full
        return 0

    lax.fori_loop(0, tiles // 4, cut, 0)
    piece_ref[...] = pc[...].astype(BF)


def back_kernel(scale, r_ref, t_ref, out_ref):
    r = r_ref[...].astype(F32)
    count = r.shape[0] // 2
    left = jnp.concatenate([r[2 * i : 2 * i + 2] for i in range(count)], axis=1).astype(BF)
    out_ref[...] = jnp.dot(left, t_ref[...], preferred_element_type=F32) * scale


def call(kernel, outs, scratch, args, smem):
    vm = pl.BlockSpec(memory_space=pltpu.VMEM)
    sm = pl.BlockSpec(memory_space=pltpu.SMEM)
    return pl.pallas_call(
        kernel,
        out_shape=outs,
        in_specs=[sm] * smem + [vm] * (len(args) - smem),
        out_specs=[vm] * len(outs),
        scratch_shapes=scratch,
        compiler_params=pltpu.CompilerParams(vmem_limit_bytes=VMEM_BYTES),
    )(*args)


def body(
    volume, back_proj, dual_state, sinogram, offsets,
    primal_first, primal_second, primal_third, dual_first, dual_second, dual_third,
):
    wide_count = lax.axis_size("wide")
    slab_count = lax.axis_size("slab")
    w = lax.axis_index("wide")
    s = lax.axis_index("slab")
    mem, zl, pix = volume.shape
    nz = zl * slab_count
    own_angles, nb = dual_state.shape[2], dual_state.shape[3]
    angles = own_angles * wide_count
    hid = primal_first.shape[4]
    scal = jnp.stack([w, s]).astype(jnp.int32)

    edge = HALO * NY
    xp = jnp.concatenate([volume, back_proj.astype(BF)[None]], axis=0).reshape((mem + 1) * zl, pix)
    from_low = shifted("wide", 1, xp[:, pix - edge :])
    from_high = shifted("wide", -1, xp[:, :edge])
    xp = jnp.concatenate([from_low, xp, from_high, jnp.zeros((xp.shape[0], 64), BF)], axis=1)
    xg = lax.all_gather(xp, "slab").reshape(-1, xp.shape[1])

    xd = jnp.concatenate([dual_state, sinogram[None]], axis=0).transpose(2, 0, 1, 3)
    xd = xd.reshape(own_angles, (mem + 1) * zl, nb)
    xd, xp = lax.optimization_barrier((xd, xp))
    xd = jnp.concatenate(
        [
            shifted("wide", 2, xd[1:]),
            shifted("wide", 1, xd),
            xd,
            shifted("wide", -1, xd),
            shifted("wide", -2, xd[:1]),
        ],
        axis=0,
    )
    xk = lax.all_gather(xd, "slab").transpose(1, 0, 2, 3).reshape(8, nz * (mem + 1), nb)

    all_z = jnp.arange(nz, dtype=jnp.int32)
    e = band(all_z, nz)
    e_slab = band(s * zl + jnp.arange(zl, dtype=jnp.int32), nz)

    def first_known(wt):
        t = jnp.einsum("yzd,dabco->yoabzc", e, wt)
        t = t.reshape(nz, hid, 3, 3, slab_count, zl, wt.shape[3]).transpose(0, 1, 2, 3, 4, 6, 5)
        return t.reshape(nz * hid, 3, 3 * nz * wt.shape[3])

    pw1 = first_known(primal_first).reshape(nz * hid, -1)
    pw2 = hidden_weights(primal_second, nz)
    third = jnp.pad(primal_third, ((0, 0),) * 4 + ((0, 1),))
    pw3 = jnp.einsum("yzd,dabco->abyozc", e, third)
    pw3 = pw3.reshape(9, slab_count, zl, mem + 1, nz * hid).transpose(0, 1, 3, 2, 4)
    pw3 = pw3.reshape(9 * nz * (mem + 1), nz * hid)

    state_sino = jnp.concatenate([dual_first[:, :, :, :mem], dual_first[:, :, :, mem + 1 :]], axis=3)
    dw1a = first_known(state_sino)
    dw1b = jnp.einsum("yzd,dabo->yoabz", e, dual_first[:, :, :, mem]).reshape(nz * hid, 3, 3 * nz)
    dw1 = jnp.concatenate([dw1a, dw1b, jnp.zeros((nz * hid, 3, 8), BF)], axis=2).reshape(nz * hid, -1)
    dw2 = hidden_weights(dual_second, nz)
    dw3 = jnp.einsum("yzd,dabco->aboyzc", e_slab, dual_third).reshape(9, mem * zl, nz * hid)
    dw3 = jnp.pad(dw3, ((0, 0), (0, 16 - mem * zl), (0, 0))).reshape(9 * 16, nz * hid)

    near_ids = w * own_angles - HALO + jnp.arange(8, dtype=jnp.int32)
    u = positions(jnp.arange(angles, dtype=jnp.int32), angles)
    u8 = positions(near_ids, angles)
    table, table8 = call(
        lambda *refs: table_kernel(angles, *refs),
        [jax.ShapeDtypeStruct((angles * BINS, pix), BF), jax.ShapeDtypeStruct((8 * BINS, pix), BF)],
        [], (u, u8), 0,
    )
    off8 = jnp.take(offsets, jnp.clip(near_ids, 0, angles - 1), axis=1)

    own, lead = call(
        lambda *refs: primal_kernel(wide_count * TX, *refs),
        [jax.ShapeDtypeStruct((mem * zl, pix), BF), jax.ShapeDtypeStruct((nz, pix), BF)],
        [
            pltpu.VMEM((9 * xg.shape[0], xg.shape[1]), BF),
            pltpu.VMEM((9 * nz * hid, xg.shape[1]), BF),
        ],
        (scal, xg, pw1, pw2, pw3), 1,
    )

    sent = jnp.broadcast_to(lead[None], (wide_count, nz, pix))
    gv = lax.all_to_all(sent, "wide", split_axis=0, concat_axis=0, tiled=True)

    k1 = dw1.shape[1] // 3
    blocks = nb // 128
    ds = dual_state.transpose(2, 0, 1, 3).reshape(own_angles, mem * zl, nb)
    nd, pieces = call(
        lambda *refs: dual_kernel(wide_count, angles, *refs),
        [
            jax.ShapeDtypeStruct((own_angles, mem * zl, nb), BF),
            jax.ShapeDtypeStruct((wide_count * zl, 128), BF),
        ],
        [
            pltpu.VMEM((wide_count * nz, 8 * BINS), F32),
            pltpu.VMEM((8, blocks + 1, 8, 128), F32),
            pltpu.VMEM((8, k1, nb), BF),
            pltpu.VMEM((6, 3 * nz * hid, nb), BF),
            pltpu.VMEM((4, nz * hid, nb), BF),
            pltpu.VMEM((4, 9 * 16, nb), F32),
            pltpu.VMEM((own_angles, blocks + 1, 8, 128), F32),
            pltpu.VMEM((wide_count * zl, 128), F32),
        ],
        (scal, off8, gv.reshape(wide_count * nz, pix), table8, xk, dw1, dw2, dw3, ds), 2,
    )
    arrived = lax.all_to_all(
        pieces.reshape(wide_count, zl, 128), "wide", split_axis=0, concat_axis=0, tiled=True
    )
    (new_back,) = call(
        lambda *refs: back_kernel(1.0 / math.sqrt(angles), *refs),
        [jax.ShapeDtypeStruct((zl, pix), F32)],
        [], (arrived.reshape(wide_count * zl, 128), table), 0,
    )
    new_dual = nd.reshape(own_angles, mem, zl, nb).transpose(1, 2, 0, 3)
    return (own.reshape(mem, zl, pix), new_dual, new_back)


def solution(mesh):
    in_specs = (
        P(None, "slab", "wide"),
        P("slab", "wide"),
        P(None, "slab", "wide", None),
        P("slab", "wide", None),
    ) + (P(),) * 7
    out_specs = (P(None, "slab", "wide"), P(None, "slab", "wide", None), P("slab", "wide"))
    return jax.shard_map(body, mesh=mesh, in_specs=in_specs, out_specs=out_specs, check_vma=False)
```

```python
import math

import jax
import jax.numpy as jnp
from jax import lax
from jax.experimental import pallas as pl
from jax.experimental.pallas import tpu as pltpu
from jax.sharding import PartitionSpec as P

NY = 32
TX = 16
BINS = NY + 2 * TX
HALO = 3
BF = jnp.bfloat16
F32 = jnp.float32


def shifted(axis, delta, value):
    size = lax.axis_size(axis)
    return lax.ppermute(value, axis, [(i, i + delta) for i in range(size) if 0 <= i + delta < size])


def band(zo, zi):
    d = jnp.arange(3, dtype=jnp.int32)
    return ((zi[None, :, None] - zo[:, None, None] + 1) == d[None, None, :]).astype(BF)


def swapped(value, mask):
    size = lax.axis_size("slab")
    return lax.ppermute(value, "slab", [(i, i ^ mask) for i in range(size)])


def hidden_base(w):
    c, o = w.shape[3], w.shape[4]
    base = w.transpose(1, 2, 4, 0, 3).reshape(9, o, 3 * c)
    return jnp.pad(base, ((0, 0), (0, 0), (0, 128 - 3 * c)))


def weights_kernel(nz, scal_ref, p_ref, d_ref, pout_ref, dout_ref):
    o = p_ref.shape[1]
    width = pout_ref.shape[1] // 9
    c = width // nz
    lane = lax.broadcasted_iota(jnp.int32, (1, width), 1)
    for tap in range(9):
        base = p_ref[tap].astype(F32)
        base = jnp.concatenate([base, jnp.zeros((o, width - base.shape[1]), F32)], axis=1)
        for zo in range(nz):
            moved = pltpu.roll(base, (c * (zo - 1)) % width, 1)
            if zo == 0:
                moved = jnp.where(lane < 2 * c, moved, 0.0)
            elif zo == nz - 1:
                moved = jnp.where(lane >= c * (zo - 1), moved, 0.0)
            pout_ref[zo * o : (zo + 1) * o, tap * width : (tap + 1) * width] = moved.astype(BF)
    count = dout_ref.shape[0] // o
    span = (count + 2) * c
    first = scal_ref[1] * 2 - 1
    for zo in range(count):
        inside = (first + zo >= 0) & (first + zo < nz)
        pieces = []
        for tap in range(9):
            base = d_ref[tap].astype(F32)
            base = jnp.concatenate([base, jnp.zeros((o, width - base.shape[1]), F32)], axis=1)
            pieces.append(pltpu.roll(base, c * zo, 1)[:, :span])
        row = jnp.where(inside, jnp.concatenate(pieces, axis=1), 0.0)
        dout_ref[zo * o : (zo + 1) * o, :] = row.astype(BF)


def table_kernel(u_ref, t_ref):
    j = lax.broadcasted_iota(jnp.int32, (BINS, TX * NY), 0).astype(F32)

    def one(a, _):
        row = u_ref[pl.ds(a, 1), :]
        t_ref[pl.ds(pl.multiple_of(a * BINS, BINS), BINS), :] = jnp.maximum(0.0, 1.0 - jnp.abs(row - j)).astype(BF)
        return 0

    lax.fori_loop(0, u_ref.shape[0], one, 0)


def positions(angle_ids, angle_total):
    angle_value = angle_ids.astype(F32) * (math.pi / angle_total)
    pixels = jnp.arange(TX * NY, dtype=jnp.int32)
    centre_x = (pixels // NY).astype(F32) - (TX - 1) / 2.0
    centre_y = (pixels % NY).astype(F32) - (NY - 1) / 2.0
    return (
        centre_x[None, :] * jnp.cos(angle_value)[:, None]
        + centre_y[None, :] * jnp.sin(angle_value)[:, None]
        + BINS / 2.0
    )


def primal_kernel(nx, scal_ref, x_ref, w1_ref, w2_ref, w3_ref, own_ref, lead_ref, col1, col2):
    lanes = x_ref.shape[1]
    lane = lax.broadcasted_iota(jnp.int32, (1, lanes), 1)
    y = lane & (NY - 1)
    gx = (lane >> 5) - HALO + scal_ref[0] * TX
    inside = (gx >= 0) & (gx < nx)

    def fill(col, value):
        rows = value.shape[0]
        for dx in range(3):
            for dy in range(3):
                shift = NY * (dx - 1) + dy - 1
                moved = value if shift == 0 else pltpu.roll(value, (-shift) % lanes, 1)
                if dy == 0:
                    moved = jnp.where(y == 0, 0.0, moved)
                elif dy == 2:
                    moved = jnp.where(y == NY - 1, 0.0, moved)
                at = (dx * 3 + dy) * rows
                col[at : at + rows, :] = moved.astype(BF)

    x = x_ref[...].astype(F32)
    fill(col1, x)
    h = jnp.dot(w1_ref[...], col1[...], preferred_element_type=F32)
    h = jnp.where(inside, jnp.maximum(h, 0.0), 0.0)
    fill(col2, h)
    h = jnp.dot(w2_ref[...], col2[...], preferred_element_type=F32)
    h = jnp.where(inside, jnp.maximum(h, 0.0), 0.0).astype(BF)
    parts = jnp.dot(w3_ref[...], h, preferred_element_type=F32)
    rows = x.shape[0]
    total = x
    for dy in range(3):
        acc = jnp.zeros((rows, lanes), F32)
        for dx in range(3):
            at = (dx * 3 + dy) * rows
            part = parts[at : at + rows, :]
            if dx != 1:
                part = pltpu.roll(part, (-NY * (dx - 1)) % lanes, 1)
            acc = acc + part
        if dy == 0:
            acc = jnp.where(y == 0, 0.0, pltpu.roll(acc, 1, 1))
        elif dy == 2:
            acc = jnp.where(y == NY - 1, 0.0, pltpu.roll(acc, lanes - 1, 1))
        total = total + acc
    total = pltpu.roll(total, lanes - HALO * NY, 1)[:, : TX * NY]
    per = rows // 4
    lead_ref[...] = jnp.concatenate([total[i * per : i * per + 2] for i in range(4)], axis=0).astype(BF)
    own_ref[...] = total[: own_ref.shape[0]].astype(BF)


def before(v):
    bins = lax.broadcasted_iota(jnp.int32, (1, v.shape[1]), 1)
    return jnp.where(bins == 0, 0.0, pltpu.roll(v, 1, 1))


def after(v):
    bins = lax.broadcasted_iota(jnp.int32, (1, v.shape[1]), 1)
    return jnp.where(bins == v.shape[1] - 1, 0.0, pltpu.roll(v, v.shape[1] - 1, 1))


def known_kernel(x0_ref, x1_ref, w_ref, out_ref, col, part, sems):
    nb = col.shape[2]
    for a in range(8):
        at = slice(a * nb, (a + 1) * nb)
        known = jnp.concatenate([x0_ref[:, at].astype(F32), x1_ref[:, at].astype(F32)], axis=0)
        col[a] = jnp.concatenate([before(known), known, after(known)], axis=0).astype(BF)
    for a in range(6):
        part[a] = jnp.dot(w_ref[...], col[a : a + 3].reshape(-1, nb), preferred_element_type=F32)
        pltpu.make_async_copy(part.at[a], out_ref.at[a], sems.at[a]).start()
    for a in range(6):
        pltpu.make_async_copy(part.at[a], out_ref.at[a], sems.at[a]).wait()


def dual_kernel(tiles, angles, *refs):
    (scal_ref, off_ref, gv_ref, t8_ref, known_ref, w1_ref, w2_ref, w3_ref, ds_ref, out_ref, piece_ref) = refs[:11]
    (win, x1, h1, h2, parts, nd, pc, known, sem) = refs[11:20]
    pj = refs[20:]
    fetch = pltpu.make_async_copy(known_ref, known, sem)
    fetch.start()
    nb = x1.shape[2]
    blocks = nb // 128
    lane = lax.broadcasted_iota(jnp.int32, (8, 128), 1)
    first_angle = scal_ref[0] * 2 - HALO

    windows = lax.dot_general(
        gv_ref[...], t8_ref[...], (((1,), (1,)), ((), ())), preferred_element_type=F32
    )
    win[...] = windows.astype(BF).astype(F32)
    for ref in pj:
        ref[...] = jnp.zeros(ref.shape, F32)

    def place(t, _):
        found = []
        for a in range(8):
            off = off_ref[t, a]
            q = off >> 7
            r = off & 127
            v = win[pl.ds(pl.multiple_of(t * 8, 8), 8), (a // 2) * 128 : (a // 2) * 128 + 128]
            moved = pltpu.roll(v, (r + 64 * (a % 2)) & 127, 1)
            lo = jnp.where((lane >= r) & (lane < r + 64), moved, 0.0)
            hi = jnp.where(lane < r - 64, moved, 0.0)
            found.append((q, pj[a][q] + lo, pj[a][q + 1] + hi))
        for a, (q, lo, hi) in enumerate(found):
            pj[a][q] = lo
            pj[a][q + 1] = hi
        return 0

    lax.fori_loop(0, tiles, place, 0)

    for a in range(8):
        valid = ((first_angle + a) >= 0) & ((first_angle + a) < angles)
        proj = jnp.concatenate([pj[a][b] for b in range(blocks)], axis=1) * (1.0 / math.sqrt(NY))
        proj = jnp.where(valid, proj, 0.0).astype(BF).astype(F32)
        x1[a] = jnp.concatenate([before(proj), proj, after(proj), jnp.zeros((8, nb), F32)], axis=0).astype(BF)

    fetch.wait()
    k1 = x1.shape[1]
    for a in range(6):
        valid = ((first_angle + a + 1) >= 0) & ((first_angle + a + 1) < angles)
        h = jnp.dot(w1_ref[...], x1[a : a + 3].reshape(3 * k1, nb), preferred_element_type=F32)
        h = jnp.where(valid, jnp.maximum(h + known[a], 0.0), 0.0)
        rows = h.shape[0]
        h1[a, 0:rows] = before(h).astype(BF)
        h1[a, rows : 2 * rows] = h.astype(BF)
        h1[a, 2 * rows : 3 * rows] = after(h).astype(BF)

    k2 = h1.shape[1]
    for a in range(4):
        valid = ((first_angle + a + 2) >= 0) & ((first_angle + a + 2) < angles)
        h = jnp.dot(w2_ref[...], h1[a : a + 3].reshape(3 * k2, nb), preferred_element_type=F32)
        h2[a] = jnp.where(valid, jnp.maximum(h, 0.0), 0.0).astype(BF)
        parts[a] = jnp.dot(w3_ref[...], h2[a], preferred_element_type=F32)

    nd[...] = jnp.zeros(nd.shape, F32)
    for a in range(2):
        acc = []
        for db in range(3):
            acc.append(sum(parts[a + da, (da * 3 + db) * 16 : (da * 3 + db) * 16 + 16] for da in range(3)))
        result = before(acc[0]) + acc[1] + after(acc[2])
        result = (ds_ref[a].astype(F32) + result[:10]).astype(BF)
        out_ref[a] = result
        lead = result.astype(F32)[:2]
        lead = jnp.concatenate([lead] * 4, axis=0)
        for b in range(blocks):
            nd[a, b] = lead[:, b * 128 : (b + 1) * 128]

    sub = lax.broadcasted_iota(jnp.int32, (8, 128), 0) >> 1

    def cut(g, _):
        full = jnp.zeros((8, 128), F32)
        for i in range(4):
            got = []
            for a in range(2):
                off = off_ref[g * 4 + i, HALO + a]
                q = off >> 7
                r = off & 127
                v = jnp.where(lane >= r, nd[a, q], nd[a, q + 1])
                got.append(pltpu.roll(v, (64 * a + 128 - r) & 127, 1))
            full = jnp.where(sub == i, jnp.where(lane < 64, got[0], got[1]), full)
        pc[pl.ds(pl.multiple_of(g * 8, 8), 8), :] = full
        return 0

    lax.fori_loop(0, tiles // 4, cut, 0)
    piece_ref[...] = pc[...].astype(BF)


def back_kernel(scale, r_ref, u_ref, out_ref):
    j = lax.broadcasted_iota(jnp.int32, (BINS, TX * NY), 0).astype(F32)
    total = jnp.zeros((8, TX * NY), F32)
    zeros = jnp.zeros((6, 128), F32)
    for i in range(r_ref.shape[0] // 4):
        r = r_ref[4 * i : 4 * i + 4, :].astype(F32)
        left = jnp.concatenate(
            [jnp.concatenate([r[0:2], zeros], axis=0), jnp.concatenate([r[2:4], zeros], axis=0)], axis=1
        ).astype(BF)
        right = jnp.concatenate(
            [jnp.maximum(0.0, 1.0 - jnp.abs(u_ref[4 * i + a : 4 * i + a + 1, :] - j)).astype(BF) for a in range(4)],
            axis=0,
        )
        total = total + jnp.dot(left, right, preferred_element_type=F32)
    out_ref[...] = total[0:2] * scale


def call(kernel, outs, scratch, args, smem, hbm_in=(), hbm_out=False, mib=24):
    vm = pl.BlockSpec(memory_space=pltpu.VMEM)
    sm = pl.BlockSpec(memory_space=pltpu.SMEM)
    hb = pl.BlockSpec(memory_space=pltpu.HBM)
    return pl.pallas_call(
        kernel,
        out_shape=outs,
        in_specs=[sm if i < smem else hb if i in hbm_in else vm for i in range(len(args))],
        out_specs=[hb if hbm_out else vm] * len(outs),
        scratch_shapes=scratch,
        compiler_params=pltpu.CompilerParams(vmem_limit_bytes=mib * 1024 * 1024),
    )(*args)


def body(
    volume, back_proj, dual_state, sinogram, offsets,
    primal_first, primal_second, primal_third, dual_first, dual_second, dual_third,
):
    wide_count = lax.axis_size("wide")
    slab_count = lax.axis_size("slab")
    w = lax.axis_index("wide")
    s = lax.axis_index("slab")
    mem, zl, pix = volume.shape
    nz = zl * slab_count
    own_angles, nb = dual_state.shape[2], dual_state.shape[3]
    angles = own_angles * wide_count
    hid = primal_first.shape[4]
    scal = jnp.stack([w, s]).astype(jnp.int32)

    rows = (mem + 1) * zl
    xp = jnp.concatenate([volume, back_proj.astype(BF)[None]], axis=0).reshape(rows, pix)
    xd = jnp.concatenate([dual_state, sinogram[None]], axis=0).transpose(0, 1, 2, 3)
    xd = xd.reshape(rows, own_angles * nb)
    both = jnp.concatenate([xp, xd], axis=1)
    both = jnp.concatenate([both, swapped(both, 2)], axis=0)
    xp, xd = both[:, :pix], both[:, pix:]
    edge = HALO * NY
    from_low = shifted("wide", 1, xp[:, pix - edge :])
    from_high = shifted("wide", -1, xp[:, :edge])
    xg = jnp.concatenate([from_low, xp, from_high, jnp.zeros((xp.shape[0], 64), BF)], axis=1)
    xg = jnp.concatenate([xg, swapped(xg, 1)], axis=0)

    all_z = jnp.arange(nz, dtype=jnp.int32)
    seen = (s ^ jnp.array([0, 2, 1, 3], jnp.int32))[:, None] * zl + jnp.arange(zl, dtype=jnp.int32)[None]
    seen = seen.reshape(nz)
    e = band(all_z, seen)
    e_out = band(seen, all_z)

    def first_known(wt, e):
        t = jnp.einsum("ypzd,dabco->yoabpcz", e.reshape(-1, slab_count, zl, 3), wt)
        return t.reshape(e.shape[0] * hid, 3, 3 * nz * wt.shape[3])

    pw1 = first_known(primal_first, e).reshape(nz * hid, -1)
    third = jnp.pad(primal_third, ((0, 0),) * 4 + ((0, 1),))
    pw3 = jnp.einsum("pyzd,dabco->abpoyzc", e_out.reshape(slab_count, zl, nz, 3), third)
    pw3 = pw3.reshape(9 * nz * (mem + 1), nz * hid)
    one, two = (zl + 4) * hid, (zl + 2) * hid
    pw2, dw2 = call(
        lambda *refs: weights_kernel(nz, *refs),
        [jax.ShapeDtypeStruct((nz * hid, 9 * nz * hid), BF), jax.ShapeDtypeStruct((two, 9 * one), BF)],
        [], (scal, hidden_base(primal_second), hidden_base(dual_second)), 1,
    )
    own, lead = call(
        lambda *refs: primal_kernel(wide_count * TX, *refs),
        [jax.ShapeDtypeStruct((mem * zl, pix), BF), jax.ShapeDtypeStruct((nz, pix), BF)],
        [
            pltpu.VMEM((9 * xg.shape[0], xg.shape[1]), BF),
            pltpu.VMEM((9 * nz * hid, xg.shape[1]), BF),
        ],
        (scal, xg, pw1, pw2, pw3), 1,
    )

    sent = jnp.broadcast_to(lead[None], (wide_count, nz, pix))
    gv = lax.all_to_all(sent, "wide", split_axis=0, concat_axis=0, tiled=True)

    xd, _ = lax.optimization_barrier((xd, lead))
    xk = jnp.concatenate(
        [
            shifted("wide", 2, xd[:, nb:]),
            shifted("wide", 1, xd),
            xd,
            shifted("wide", -1, xd),
            shifted("wide", -2, xd[:, :nb]),
        ],
        axis=1,
    )
    xk = (xk, swapped(xk, 1))
    z_one = s * zl - 2 + jnp.arange(zl + 4, dtype=jnp.int32)
    z_two = s * zl - 1 + jnp.arange(zl + 2, dtype=jnp.int32)
    z_own = s * zl + jnp.arange(zl, dtype=jnp.int32)
    def inside_z(z):
        return ((z >= 0) & (z < nz)).astype(BF)[:, None, None]

    e_one = band(z_one, seen) * inside_z(z_one)
    state_sino = jnp.concatenate([dual_first[:, :, :, :mem], dual_first[:, :, :, mem + 1 :]], axis=3)
    dw1a = first_known(state_sino, e_one).reshape(one, -1)
    dw1b = jnp.einsum("yzd,dabo->yoabz", e_one, dual_first[:, :, :, mem]).reshape(one, 3, 3 * nz)
    dw1b = jnp.pad(dw1b, ((0, 0), (0, 0), (0, 8))).reshape(one, -1)
    dw3 = jnp.einsum("yzd,dabco->aboyzc", band(z_own, z_two), dual_third).reshape(9, mem * zl, two)
    dw3 = jnp.pad(dw3, ((0, 0), (0, 16 - mem * zl), (0, 0))).reshape(9 * 16, two)
    (known,) = call(
        known_kernel, [jax.ShapeDtypeStruct((6, one, nb), F32)],
        [pltpu.VMEM((8, 3 * nz * (mem + 1), nb), BF), pltpu.VMEM((6, one, nb), F32), pltpu.SemaphoreType.DMA((6,))],
        (*xk, dw1a), 0, hbm_out=True, mib=60,
    )

    near_ids = w * own_angles - HALO + jnp.arange(8, dtype=jnp.int32)
    (table8,) = call(
        table_kernel, [jax.ShapeDtypeStruct((8 * BINS, pix), BF)], [], (positions(near_ids, angles),), 0
    )
    off8 = jnp.take(offsets, jnp.clip(near_ids, 0, angles - 1), axis=1)

    blocks = nb // 128
    ds = dual_state.transpose(2, 0, 1, 3).reshape(own_angles, mem * zl, nb)
    nd, pieces = call(
        lambda *refs: dual_kernel(wide_count, angles, *refs),
        [
            jax.ShapeDtypeStruct((own_angles, mem * zl, nb), BF),
            jax.ShapeDtypeStruct((wide_count * zl, 128), BF),
        ],
        [
            pltpu.VMEM((wide_count * nz, 8 * BINS), F32),
            pltpu.VMEM((8, 4 * 8, nb), BF),
            pltpu.VMEM((6, 3 * one, nb), BF),
            pltpu.VMEM((4, two, nb), BF),
            pltpu.VMEM((4, 9 * 16, nb), F32),
            pltpu.VMEM((own_angles, blocks + 1, 8, 128), F32),
            pltpu.VMEM((wide_count * zl, 128), F32),
            pltpu.VMEM((6, one, nb), F32),
            pltpu.SemaphoreType.DMA,
        ]
        + [pltpu.VMEM((blocks + 1, 8, 128), F32)] * 8,
        (scal, off8, gv.reshape(wide_count * nz, pix), table8, known, dw1b, dw2, dw3, ds), 2, hbm_in=(4,), mib=60,
    )
    arrived = lax.all_to_all(
        pieces.reshape(wide_count, zl, 128), "wide", split_axis=0, concat_axis=0, tiled=True
    )
    (new_back,) = call(
        lambda *refs: back_kernel(1.0 / math.sqrt(angles), *refs), [jax.ShapeDtypeStruct((zl, pix), F32)],
        [], (arrived.reshape(wide_count * zl, 128), positions(jnp.arange(angles, dtype=jnp.int32), angles)), 0,
    )
    new_dual = nd.reshape(own_angles, mem, zl, nb).transpose(1, 2, 0, 3)
    return (own.reshape(mem, zl, pix), new_dual, new_back)


def solution(mesh):
    in_specs = (
        P(None, "slab", "wide"),
        P("slab", "wide"),
        P(None, "slab", "wide", None),
        P("slab", "wide", None),
    ) + (P(),) * 7
    out_specs = (P(None, "slab", "wide"), P(None, "slab", "wide", None), P("slab", "wide"))
    return jax.shard_map(body, mesh=mesh, in_specs=in_specs, out_specs=out_specs, check_vma=False)
```

```python
import math

import jax
import jax.numpy as jnp
from jax import lax
from jax.experimental import pallas as pl
from jax.experimental.pallas import tpu as pltpu
from jax.sharding import PartitionSpec as P

NY = 32
TX = 16
BINS = NY + 2 * TX
HALO = 3
BF = jnp.bfloat16
F32 = jnp.float32


def shifted(axis, delta, value):
    size = lax.axis_size(axis)
    return lax.ppermute(value, axis, [(i, i + delta) for i in range(size) if 0 <= i + delta < size])


def band(zo, zi):
    d = jnp.arange(3, dtype=jnp.int32)
    return ((zi[None, :, None] - zo[:, None, None] + 1) == d[None, None, :]).astype(BF)


def swapped(value, mask):
    size = lax.axis_size("slab")
    return lax.ppermute(value, "slab", [(i, i ^ mask) for i in range(size)])


def hidden_base(w):
    c, o = w.shape[3], w.shape[4]
    base = w.transpose(1, 2, 4, 0, 3).reshape(9, o, 3 * c)
    return jnp.pad(base, ((0, 0), (0, 0), (0, 128 - 3 * c)))


def primal_weights_kernel(nz, p_ref, pout_ref):
    o = p_ref.shape[1]
    width = pout_ref.shape[1] // 9
    c = width // nz
    lane = lax.broadcasted_iota(jnp.int32, (1, width), 1)
    for tap in range(9):
        base = p_ref[tap].astype(F32)
        base = jnp.concatenate([base, jnp.zeros((o, width - base.shape[1]), F32)], axis=1)
        for zo in range(nz):
            moved = pltpu.roll(base, (c * (zo - 1)) % width, 1)
            if zo == 0:
                moved = jnp.where(lane < 2 * c, moved, 0.0)
            elif zo == nz - 1:
                moved = jnp.where(lane >= c * (zo - 1), moved, 0.0)
            pout_ref[zo * o : (zo + 1) * o, tap * width : (tap + 1) * width] = moved.astype(BF)


def dual_weights_kernel(nz, scal_ref, d_ref, dout_ref):
    o = d_ref.shape[1]
    c = dout_ref.shape[1] // 9 // (dout_ref.shape[0] // o + 2)
    width = 256
    count = dout_ref.shape[0] // o
    span = (count + 2) * c
    first = scal_ref[1] * 2 - 1
    for zo in range(count):
        inside = (first + zo >= 0) & (first + zo < nz)
        pieces = []
        for tap in range(9):
            base = d_ref[tap].astype(F32)
            base = jnp.concatenate([base, jnp.zeros((o, width - base.shape[1]), F32)], axis=1)
            pieces.append(pltpu.roll(base, c * zo, 1)[:, :span])
        row = jnp.where(inside, jnp.concatenate(pieces, axis=1), 0.0)
        dout_ref[zo * o : (zo + 1) * o, :] = row.astype(BF)


def table_kernel(u_ref, t_ref):
    j = lax.broadcasted_iota(jnp.int32, (BINS, TX * NY), 0).astype(F32)

    def one(a, _):
        row = u_ref[pl.ds(a, 1), :]
        t_ref[pl.ds(pl.multiple_of(a * BINS, BINS), BINS), :] = jnp.maximum(0.0, 1.0 - jnp.abs(row - j)).astype(BF)
        return 0

    lax.fori_loop(0, u_ref.shape[0], one, 0)


def positions(angle_ids, angle_total, first_pixel=0):
    angle_value = angle_ids.astype(F32) * (math.pi / angle_total)
    pixels = (jnp.arange(TX * NY, dtype=jnp.int32) + first_pixel) % (TX * NY)
    centre_x = (pixels // NY).astype(F32) - (TX - 1) / 2.0
    centre_y = (pixels % NY).astype(F32) - (NY - 1) / 2.0
    return (
        centre_x[None, :] * jnp.cos(angle_value)[:, None]
        + centre_y[None, :] * jnp.sin(angle_value)[:, None]
        + BINS / 2.0
    )


def primal_kernel(nx, scal_ref, x_ref, w1_ref, w2_ref, w3_ref, own_ref, lead_ref, col1, col2):
    lanes = x_ref.shape[1]
    lane = lax.broadcasted_iota(jnp.int32, (1, lanes), 1)
    y = lane & (NY - 1)
    gx = (lane >> 5) - HALO + scal_ref[0] * TX
    inside = (gx >= 0) & (gx < nx)

    def fill(col, value):
        rows = value.shape[0]
        for dx in range(3):
            for dy in range(3):
                shift = NY * (dx - 1) + dy - 1
                moved = value if shift == 0 else pltpu.roll(value, (-shift) % lanes, 1)
                if dy == 0:
                    moved = jnp.where(y == 0, 0.0, moved)
                elif dy == 2:
                    moved = jnp.where(y == NY - 1, 0.0, moved)
                at = (dx * 3 + dy) * rows
                col[at : at + rows, :] = moved.astype(BF)

    x = x_ref[...].astype(F32)
    fill(col1, x)
    h = jnp.dot(w1_ref[...], col1[...], preferred_element_type=F32)
    h = jnp.where(inside, jnp.maximum(h, 0.0), 0.0)
    fill(col2, h)
    h = jnp.dot(w2_ref[...], col2[...], preferred_element_type=F32)
    h = jnp.where(inside, jnp.maximum(h, 0.0), 0.0).astype(BF)
    parts = jnp.dot(w3_ref[...], h, preferred_element_type=F32)
    rows = x.shape[0]
    total = x
    for dy in range(3):
        acc = jnp.zeros((rows, lanes), F32)
        for dx in range(3):
            at = (dx * 3 + dy) * rows
            part = parts[at : at + rows, :]
            if dx != 1:
                part = pltpu.roll(part, (-NY * (dx - 1)) % lanes, 1)
            acc = acc + part
        if dy == 0:
            acc = jnp.where(y == 0, 0.0, pltpu.roll(acc, 1, 1))
        elif dy == 2:
            acc = jnp.where(y == NY - 1, 0.0, pltpu.roll(acc, lanes - 1, 1))
        total = total + acc
    total = pltpu.roll(total, lanes - HALO * NY, 1)[:, : TX * NY]
    per = rows // 4
    lead = jnp.concatenate([total[i * per : i * per + 2] for i in range(4)], axis=0)
    lead = jnp.where((scal_ref[1] & 1) == 0, lead, pltpu.roll(lead, 4, 0))
    half = TX * NY // 2
    lead_ref[...] = jnp.where((scal_ref[1] & 1) == 0, lead[:, :half], lead[:, half:]).astype(BF)
    own_ref[...] = total[: own_ref.shape[0]].astype(BF)


def before(v):
    bins = lax.broadcasted_iota(jnp.int32, (1, v.shape[1]), 1)
    return jnp.where(bins == 0, 0.0, pltpu.roll(v, 1, 1))


def after(v):
    bins = lax.broadcasted_iota(jnp.int32, (1, v.shape[1]), 1)
    return jnp.where(bins == v.shape[1] - 1, 0.0, pltpu.roll(v, v.shape[1] - 1, 1))


def dual_kernel(tiles, angles, *refs):
    (scal_ref, off_ref, g0_ref, g1_ref, t8_ref, xa_ref, xb_ref, w1_ref, w2_ref, w3_ref, ds_ref, out_ref, piece_ref) = refs[:13]
    (win, x1, h1, h2, parts, nd, pc) = refs[13:20]
    pj = refs[20:]
    nb = x1.shape[2]
    blocks = nb // 128
    lane = lax.broadcasted_iota(jnp.int32, (8, 128), 1)
    first_angle = scal_ref[0] * 2 - HALO

    half = g0_ref.shape[1]
    windows = sum(
        lax.dot_general(ref[...], t8_ref[:, at : at + half], (((1,), (1,)), ((), ())), preferred_element_type=F32)
        for ref, at in ((g0_ref, 0), (g1_ref, half))
    )
    win[...] = windows.astype(BF).astype(F32)
    for ref in pj:
        ref[...] = jnp.zeros(ref.shape, F32)

    def place(t, _):
        found = []
        for a in range(8):
            off = off_ref[t, a]
            q = off >> 7
            r = off & 127
            v = win[pl.ds(pl.multiple_of(t * 8, 8), 8), (a // 2) * 128 : (a // 2) * 128 + 128]
            moved = pltpu.roll(v, (r + 64 * (a % 2)) & 127, 1)
            lo = jnp.where((lane >= r) & (lane < r + 64), moved, 0.0)
            hi = jnp.where(lane < r - 64, moved, 0.0)
            found.append((q, pj[a][q] + lo, pj[a][q + 1] + hi))
        for a, (q, lo, hi) in enumerate(found):
            pj[a][q] = lo
            pj[a][q + 1] = hi
        return 0

    lax.fori_loop(0, tiles, place, 0)

    for a in range(8):
        valid = ((first_angle + a) >= 0) & ((first_angle + a) < angles)
        proj = jnp.concatenate([pj[a][b] for b in range(blocks)], axis=1) * (1.0 / math.sqrt(NY))
        proj = jnp.where(valid, proj, 0.0).astype(BF).astype(F32)
        at = slice(a * nb, (a + 1) * nb)
        known = jnp.concatenate([xa_ref[:, at].astype(F32), xb_ref[:, at].astype(F32)], axis=0)
        x1[a] = jnp.concatenate(
            [before(known), known, after(known), before(proj), proj, after(proj), jnp.zeros((8, nb), F32)], axis=0
        ).astype(BF)

    k1 = x1.shape[1]
    for a in range(6):
        valid = ((first_angle + a + 1) >= 0) & ((first_angle + a + 1) < angles)
        h = jnp.dot(w1_ref[...], x1[a : a + 3].reshape(3 * k1, nb), preferred_element_type=F32)
        h = jnp.where(valid, jnp.maximum(h, 0.0), 0.0)
        rows = h.shape[0]
        h1[a, 0:rows] = before(h).astype(BF)
        h1[a, rows : 2 * rows] = h.astype(BF)
        h1[a, 2 * rows : 3 * rows] = after(h).astype(BF)

    k2 = h1.shape[1]
    for a in range(4):
        valid = ((first_angle + a + 2) >= 0) & ((first_angle + a + 2) < angles)
        h = jnp.dot(w2_ref[...], h1[a : a + 3].reshape(3 * k2, nb), preferred_element_type=F32)
        h2[a] = jnp.where(valid, jnp.maximum(h, 0.0), 0.0).astype(BF)
        parts[a] = jnp.dot(w3_ref[...], h2[a], preferred_element_type=F32)

    nd[...] = jnp.zeros(nd.shape, F32)
    for a in range(2):
        acc = []
        for db in range(3):
            acc.append(sum(parts[a + da, (da * 3 + db) * 16 : (da * 3 + db) * 16 + 16] for da in range(3)))
        result = before(acc[0]) + acc[1] + after(acc[2])
        result = (ds_ref[a].astype(F32) + result[:10]).astype(BF)
        out_ref[a] = result
        lead = result.astype(F32)[:2]
        lead = jnp.concatenate([lead] * 4, axis=0)
        for b in range(blocks):
            nd[a, b] = lead[:, b * 128 : (b + 1) * 128]

    sub = lax.broadcasted_iota(jnp.int32, (8, 128), 0) >> 1

    def cut(g, _):
        full = jnp.zeros((8, 128), F32)
        for i in range(4):
            got = []
            for a in range(2):
                off = off_ref[g * 4 + i, HALO + a]
                q = off >> 7
                r = off & 127
                v = jnp.where(lane >= r, nd[a, q], nd[a, q + 1])
                got.append(pltpu.roll(v, (64 * a + 128 - r) & 127, 1))
            full = jnp.where(sub == i, jnp.where(lane < 64, got[0], got[1]), full)
        pc[pl.ds(pl.multiple_of(g * 8, 8), 8), :] = full
        return 0

    lax.fori_loop(0, tiles // 4, cut, 0)
    piece_ref[...] = pc[...].astype(BF)


def back_kernel(scale, r_ref, u_ref, out_ref):
    j = lax.broadcasted_iota(jnp.int32, (BINS, TX * NY), 0).astype(F32)
    total = jnp.zeros((8, TX * NY), F32)
    zeros = jnp.zeros((6, 128), F32)
    for i in range(r_ref.shape[0] // 4):
        r = r_ref[4 * i : 4 * i + 4, :].astype(F32)
        left = jnp.concatenate(
            [jnp.concatenate([r[0:2], zeros], axis=0), jnp.concatenate([r[2:4], zeros], axis=0)], axis=1
        ).astype(BF)
        right = jnp.concatenate(
            [jnp.maximum(0.0, 1.0 - jnp.abs(u_ref[4 * i + a : 4 * i + a + 1, :] - j)).astype(BF) for a in range(4)],
            axis=0,
        )
        total = total + jnp.dot(left, right, preferred_element_type=F32)
    out_ref[...] = total[0:2] * scale


def call(kernel, outs, scratch, args, smem, mib=24):
    vm = pl.BlockSpec(memory_space=pltpu.VMEM)
    sm = pl.BlockSpec(memory_space=pltpu.SMEM)
    return pl.pallas_call(
        kernel,
        out_shape=outs,
        in_specs=[sm] * smem + [vm] * (len(args) - smem),
        out_specs=[vm] * len(outs),
        scratch_shapes=scratch,
        compiler_params=pltpu.CompilerParams(vmem_limit_bytes=mib * 1024 * 1024),
    )(*args)


def body(
    volume, back_proj, dual_state, sinogram, offsets,
    primal_first, primal_second, primal_third, dual_first, dual_second, dual_third,
):
    wide_count = lax.axis_size("wide")
    slab_count = lax.axis_size("slab")
    w = lax.axis_index("wide")
    s = lax.axis_index("slab")
    mem, zl, pix = volume.shape
    nz = zl * slab_count
    own_angles, nb = dual_state.shape[2], dual_state.shape[3]
    angles = own_angles * wide_count
    hid = primal_first.shape[4]
    scal = jnp.stack([w, s]).astype(jnp.int32)

    rows = (mem + 1) * zl
    xp = jnp.concatenate([volume, back_proj.astype(BF)[None]], axis=0).reshape(rows, pix)
    xd = jnp.concatenate([dual_state, sinogram[None]], axis=0).transpose(0, 1, 2, 3)
    xd = xd.reshape(rows, own_angles * nb)
    both = jnp.concatenate([xp, xd], axis=1)
    both = jnp.concatenate([both, swapped(both, 2)], axis=0)
    xp, xd = both[:, :pix], both[:, pix:]
    edge = HALO * NY
    from_low = shifted("wide", 1, xp[:, pix - edge :])
    from_high = shifted("wide", -1, xp[:, :edge])
    xg = jnp.concatenate([from_low, xp, from_high, jnp.zeros((xp.shape[0], 64), BF)], axis=1)
    xg = jnp.concatenate([xg, swapped(xg, 1)], axis=0)

    all_z = jnp.arange(nz, dtype=jnp.int32)
    def z_order(slab):
        slabs = slab ^ jnp.array([0, 2, 1, 3], jnp.int32)
        return (slabs[:, None] * zl + jnp.arange(zl, dtype=jnp.int32)[None]).reshape(nz)

    seen = z_order(s)
    lead_z = z_order(s & 2)
    e = band(all_z, seen)
    e_out = band(seen, all_z)

    def first_known(wt, e):
        t = jnp.einsum("ypzd,dabco->yoabpcz", e.reshape(-1, slab_count, zl, 3), wt)
        return t.reshape(e.shape[0] * hid, 3, 3 * nz * wt.shape[3])

    pw1 = first_known(primal_first, e).reshape(nz * hid, -1)
    third = jnp.pad(primal_third, ((0, 0),) * 4 + ((0, 1),))
    pw3 = jnp.einsum("pyzd,dabco->abpoyzc", e_out.reshape(slab_count, zl, nz, 3), third)
    pw3 = pw3.reshape(9 * nz * (mem + 1), nz * hid)
    one, two = (zl + 4) * hid, (zl + 2) * hid
    (pw2,) = call(
        lambda *refs: primal_weights_kernel(nz, *refs),
        [jax.ShapeDtypeStruct((nz * hid, 9 * nz * hid), BF)], [], (hidden_base(primal_second),), 0,
    )
    own, lead = call(
        lambda *refs: primal_kernel(wide_count * TX, *refs),
        [jax.ShapeDtypeStruct((mem * zl, pix), BF), jax.ShapeDtypeStruct((nz, pix // 2), BF)],
        [
            pltpu.VMEM((9 * xg.shape[0], xg.shape[1]), BF),
            pltpu.VMEM((9 * nz * hid, xg.shape[1]), BF),
        ],
        (scal, xg, pw1, pw2, pw3), 1,
    )

    sent = jnp.broadcast_to(lead[None], (wide_count, nz, pix // 2))
    gv = lax.all_to_all(sent, "wide", split_axis=0, concat_axis=0, tiled=True)
    gv = gv.reshape(wide_count * nz, pix // 2)

    xd, _ = lax.optimization_barrier((xd, lead))
    xk = jnp.concatenate(
        [
            shifted("wide", 2, xd[:, nb:]),
            shifted("wide", 1, xd),
            xd,
            shifted("wide", -1, xd),
            shifted("wide", -2, xd[:, :nb]),
        ],
        axis=1,
    )
    xk, dual_first, dual_second, dual_third, w, offsets = lax.optimization_barrier(
        (xk, dual_first, dual_second, dual_third, w, offsets)
    )
    (dw2,) = call(
        lambda *refs: dual_weights_kernel(nz, *refs),
        [jax.ShapeDtypeStruct((two, 9 * one), BF)], [], (scal, hidden_base(dual_second)), 1,
    )
    z_one = s * zl - 2 + jnp.arange(zl + 4, dtype=jnp.int32)
    z_two = s * zl - 1 + jnp.arange(zl + 2, dtype=jnp.int32)
    z_own = s * zl + jnp.arange(zl, dtype=jnp.int32)
    def inside_z(z):
        return ((z >= 0) & (z < nz)).astype(BF)[:, None, None]

    e_one = band(z_one, seen) * inside_z(z_one)
    state_sino = jnp.concatenate([dual_first[:, :, :, :mem], dual_first[:, :, :, mem + 1 :]], axis=3)
    dw1a = first_known(state_sino, e_one)
    e_lead = band(z_one, lead_z) * inside_z(z_one)
    dw1b = jnp.einsum("yzd,dabo->yoabz", e_lead, dual_first[:, :, :, mem]).reshape(one, 3, 3 * nz)
    dw1 = jnp.concatenate([dw1a, dw1b, jnp.zeros((one, 3, 8), BF)], axis=2).reshape(one, -1)
    dw3 = jnp.einsum("yzd,dabco->aboyzc", band(z_own, z_two), dual_third).reshape(9, mem * zl, two)
    dw3 = jnp.pad(dw3, ((0, 0), (0, 16 - mem * zl), (0, 0))).reshape(9 * 16, two)
    near_ids = w * own_angles - HALO + jnp.arange(8, dtype=jnp.int32)
    (table8,) = call(
        table_kernel, [jax.ShapeDtypeStruct((8 * BINS, pix), BF)], [], (positions(near_ids, angles, (s & 1) * (pix // 2)),), 0
    )
    off8 = jnp.take(offsets, jnp.clip(near_ids, 0, angles - 1), axis=1)

    blocks = nb // 128
    ds = dual_state.transpose(2, 0, 1, 3).reshape(own_angles, mem * zl, nb)
    gv, xk, off8, table8, dw1, dw2, dw3, ds = lax.optimization_barrier(
        (gv, xk, off8, table8, dw1, dw2, dw3, ds)
    )
    gv = (gv, swapped(gv, 1))
    xk = (xk, swapped(xk, 1))
    nd, pieces = call(
        lambda *refs: dual_kernel(wide_count, angles, *refs),
        [
            jax.ShapeDtypeStruct((own_angles, mem * zl, nb), BF),
            jax.ShapeDtypeStruct((wide_count * zl, 128), BF),
        ],
        [
            pltpu.VMEM((wide_count * nz, 8 * BINS), F32),
            pltpu.VMEM((8, dw1.shape[1] // 3, nb), BF),
            pltpu.VMEM((6, 3 * one, nb), BF),
            pltpu.VMEM((4, two, nb), BF),
            pltpu.VMEM((4, 9 * 16, nb), F32),
            pltpu.VMEM((own_angles, blocks + 1, 8, 128), F32),
            pltpu.VMEM((wide_count * zl, 128), F32),
        ]
        + [pltpu.VMEM((blocks + 1, 8, 128), F32)] * 8,
        (scal, off8, *gv, table8, *xk, dw1, dw2, dw3, ds), 2, mib=32,
    )
    arrived = lax.all_to_all(
        pieces.reshape(wide_count, zl, 128), "wide", split_axis=0, concat_axis=0, tiled=True
    )
    (new_back,) = call(
        lambda *refs: back_kernel(1.0 / math.sqrt(angles), *refs), [jax.ShapeDtypeStruct((zl, pix), F32)],
        [], (arrived.reshape(wide_count * zl, 128), positions(jnp.arange(angles, dtype=jnp.int32), angles)), 0,
    )
    new_dual = nd.reshape(own_angles, mem, zl, nb).transpose(1, 2, 0, 3)
    return (own.reshape(mem, zl, pix), new_dual, new_back)


def solution(mesh):
    in_specs = (
        P(None, "slab", "wide"),
        P("slab", "wide"),
        P(None, "slab", "wide", None),
        P("slab", "wide", None),
    ) + (P(),) * 7
    out_specs = (P(None, "slab", "wide"), P(None, "slab", "wide", None), P("slab", "wide"))
    return jax.shard_map(body, mesh=mesh, in_specs=in_specs, out_specs=out_specs, check_vma=False)
```

```python
import math

import jax
import jax.numpy as jnp
from jax import lax
from jax.experimental import pallas as pl
from jax.experimental.pallas import tpu as pltpu
from jax.sharding import PartitionSpec as P

NY = 32
TX = 16
BINS = NY + 2 * TX
HALO = 3
BF = jnp.bfloat16
F32 = jnp.float32


def shifted(axis, delta, value):
    size = lax.axis_size(axis)
    return lax.ppermute(value, axis, [(i, i + delta) for i in range(size) if 0 <= i + delta < size])


def band(zo, zi):
    d = jnp.arange(3, dtype=jnp.int32)
    return ((zi[None, :, None] - zo[:, None, None] + 1) == d[None, None, :]).astype(BF)


def from_sides(value, distance):
    wide, slab = lax.axis_size("wide"), lax.axis_size("slab")
    pairs = []
    for i in range(wide):
        for j in range(slab):
            to = i - distance if j % 2 else i + distance
            if 0 <= to < wide:
                pairs.append((i * slab + j, to * slab + j))
    return lax.ppermute(value, ("wide", "slab"), pairs)


def swapped(value, mask):
    size = lax.axis_size("slab")
    return lax.ppermute(value, "slab", [(i, i ^ mask) for i in range(size)])


def hidden_base(w):
    c, o = w.shape[3], w.shape[4]
    base = w.transpose(1, 2, 4, 0, 3).reshape(9, o, 3 * c)
    return jnp.pad(base, ((0, 0), (0, 0), (0, 128 - 3 * c)))


def primal_weights_kernel(nz, p_ref, pout_ref):
    o = p_ref.shape[1]
    width = pout_ref.shape[1] // 9
    c = width // nz
    lane = lax.broadcasted_iota(jnp.int32, (1, width), 1)
    for tap in range(9):
        base = p_ref[tap].astype(F32)
        base = jnp.concatenate([base, jnp.zeros((o, width - base.shape[1]), F32)], axis=1)
        for zo in range(nz):
            moved = pltpu.roll(base, (c * (zo - 1)) % width, 1)
            if zo == 0:
                moved = jnp.where(lane < 2 * c, moved, 0.0)
            elif zo == nz - 1:
                moved = jnp.where(lane >= c * (zo - 1), moved, 0.0)
            pout_ref[zo * o : (zo + 1) * o, tap * width : (tap + 1) * width] = moved.astype(BF)


def dual_weights_kernel(nz, scal_ref, d_ref, dout_ref):
    o = d_ref.shape[1]
    c = dout_ref.shape[1] // 9 // (dout_ref.shape[0] // o + 2)
    width = 256
    count = dout_ref.shape[0] // o
    span = (count + 2) * c
    first = scal_ref[1] * 2 - 1
    for zo in range(count):
        inside = (first + zo >= 0) & (first + zo < nz)
        pieces = []
        for tap in range(9):
            base = d_ref[tap].astype(F32)
            base = jnp.concatenate([base, jnp.zeros((o, width - base.shape[1]), F32)], axis=1)
            pieces.append(pltpu.roll(base, c * zo, 1)[:, :span])
        row = jnp.where(inside, jnp.concatenate(pieces, axis=1), 0.0)
        dout_ref[zo * o : (zo + 1) * o, :] = row.astype(BF)


def table_kernel(u_ref, t_ref):
    j = lax.broadcasted_iota(jnp.int32, (BINS, TX * NY), 0).astype(F32)

    def one(a, _):
        row = u_ref[pl.ds(a, 1), :]
        t_ref[pl.ds(pl.multiple_of(a * BINS, BINS), BINS), :] = jnp.maximum(0.0, 1.0 - jnp.abs(row - j)).astype(BF)
        return 0

    lax.fori_loop(0, u_ref.shape[0], one, 0)


def positions(angle_ids, angle_total, first_pixel=0):
    angle_value = angle_ids.astype(F32) * (math.pi / angle_total)
    pixels = (jnp.arange(TX * NY, dtype=jnp.int32) + first_pixel) % (TX * NY)
    centre_x = (pixels // NY).astype(F32) - (TX - 1) / 2.0
    centre_y = (pixels % NY).astype(F32) - (NY - 1) / 2.0
    return (
        centre_x[None, :] * jnp.cos(angle_value)[:, None]
        + centre_y[None, :] * jnp.sin(angle_value)[:, None]
        + BINS / 2.0
    )


def primal_kernel(nx, scal_ref, x_ref, w1_ref, w2_ref, w3_ref, own_ref, lead_ref, col1, col2):
    lanes = x_ref.shape[1]
    lane = lax.broadcasted_iota(jnp.int32, (1, lanes), 1)
    y = lane & (NY - 1)
    gx = (lane >> 5) - HALO + scal_ref[0] * TX
    inside = (gx >= 0) & (gx < nx)

    def fill(col, value):
        rows = value.shape[0]
        for dx in range(3):
            for dy in range(3):
                shift = NY * (dx - 1) + dy - 1
                moved = value if shift == 0 else pltpu.roll(value, (-shift) % lanes, 1)
                if dy == 0:
                    moved = jnp.where(y == 0, 0.0, moved)
                elif dy == 2:
                    moved = jnp.where(y == NY - 1, 0.0, moved)
                at = (dx * 3 + dy) * rows
                col[at : at + rows, :] = moved.astype(BF)

    x = x_ref[...].astype(F32)
    fill(col1, x)
    h = jnp.dot(w1_ref[...], col1[...], preferred_element_type=F32)
    h = jnp.where(inside, jnp.maximum(h, 0.0), 0.0)
    fill(col2, h)
    h = jnp.dot(w2_ref[...], col2[...], preferred_element_type=F32)
    h = jnp.where(inside, jnp.maximum(h, 0.0), 0.0).astype(BF)
    parts = jnp.dot(w3_ref[...], h, preferred_element_type=F32)
    rows = x.shape[0]
    total = x
    for dy in range(3):
        acc = jnp.zeros((rows, lanes), F32)
        for dx in range(3):
            at = (dx * 3 + dy) * rows
            part = parts[at : at + rows, :]
            if dx != 1:
                part = pltpu.roll(part, (-NY * (dx - 1)) % lanes, 1)
            acc = acc + part
        if dy == 0:
            acc = jnp.where(y == 0, 0.0, pltpu.roll(acc, 1, 1))
        elif dy == 2:
            acc = jnp.where(y == NY - 1, 0.0, pltpu.roll(acc, lanes - 1, 1))
        total = total + acc
    total = pltpu.roll(total, lanes - HALO * NY, 1)[:, : TX * NY]
    per = rows // 4
    lead = jnp.concatenate([total[i * per : i * per + 2] for i in range(4)], axis=0)
    lead = jnp.where((scal_ref[1] & 1) == 0, lead, pltpu.roll(lead, 4, 0))
    half = TX * NY // 2
    lead_ref[...] = jnp.where((scal_ref[1] & 1) == 0, lead[:, :half], lead[:, half:]).astype(BF)
    own_ref[...] = total[: own_ref.shape[0]].astype(BF)


def before(v):
    bins = lax.broadcasted_iota(jnp.int32, (1, v.shape[1]), 1)
    return jnp.where(bins == 0, 0.0, pltpu.roll(v, 1, 1))


def after(v):
    bins = lax.broadcasted_iota(jnp.int32, (1, v.shape[1]), 1)
    return jnp.where(bins == v.shape[1] - 1, 0.0, pltpu.roll(v, v.shape[1] - 1, 1))


def dual_kernel(tiles, angles, *refs):
    (scal_ref, off_ref, g0_ref, g1_ref, t8_ref, xo_ref, xa_ref, xb_ref, w1_ref, w2_ref, w3_ref, ds_ref, out_ref, piece_ref) = refs[:14]
    (win, x1, h1, h2, parts, nd, pc) = refs[14:21]
    pj = refs[21:]
    nb = x1.shape[2]
    blocks = nb // 128
    lane = lax.broadcasted_iota(jnp.int32, (8, 128), 1)
    first_angle = scal_ref[0] * 2 - HALO

    half = g0_ref.shape[1]
    windows = sum(
        lax.dot_general(ref[...], t8_ref[:, at : at + half], (((1,), (1,)), ((), ())), preferred_element_type=F32)
        for ref, at in ((g0_ref, 0), (g1_ref, half))
    )
    win[...] = windows.astype(BF).astype(F32)
    for ref in pj:
        ref[...] = jnp.zeros(ref.shape, F32)

    def place(t, _):
        found = []
        for a in range(8):
            off = off_ref[t, a]
            q = off >> 7
            r = off & 127
            v = win[pl.ds(pl.multiple_of(t * 8, 8), 8), (a // 2) * 128 : (a // 2) * 128 + 128]
            moved = pltpu.roll(v, (r + 64 * (a % 2)) & 127, 1)
            lo = jnp.where((lane >= r) & (lane < r + 64), moved, 0.0)
            hi = jnp.where(lane < r - 64, moved, 0.0)
            found.append((q, pj[a][q] + lo, pj[a][q + 1] + hi))
        for a, (q, lo, hi) in enumerate(found):
            pj[a][q] = lo
            pj[a][q + 1] = hi
        return 0

    lax.fori_loop(0, tiles, place, 0)

    low_core = (scal_ref[1] & 1) == 0
    for a in range(8):
        valid = ((first_angle + a) >= 0) & ((first_angle + a) < angles)
        proj = jnp.concatenate([pj[a][b] for b in range(blocks)], axis=1) * (1.0 / math.sqrt(NY))
        proj = jnp.where(valid, proj, 0.0).astype(BF).astype(F32)
        if a in (3, 4):
            known = xo_ref[:, (a - 3) * nb : (a - 2) * nb].astype(F32)
        else:
            at = {0: 2, 1: 0, 2: 1, 5: 0, 6: 1, 7: 2}[a] * nb
            mine = xa_ref[:, at : at + nb].astype(F32)
            theirs = xb_ref[:, at : at + nb].astype(F32)
            theirs = jnp.concatenate([theirs[theirs.shape[0] // 2 :], theirs[: theirs.shape[0] // 2]], axis=0)
            known = jnp.where(low_core, mine, theirs) if a < 3 else jnp.where(low_core, theirs, mine)
        x1[a] = jnp.concatenate(
            [before(known), known, after(known), before(proj), proj, after(proj), jnp.zeros((8, nb), F32)], axis=0
        ).astype(BF)

    k1 = x1.shape[1]
    for a in range(6):
        valid = ((first_angle + a + 1) >= 0) & ((first_angle + a + 1) < angles)
        h = jnp.dot(w1_ref[...], x1[a : a + 3].reshape(3 * k1, nb), preferred_element_type=F32)
        h = jnp.where(valid, jnp.maximum(h, 0.0), 0.0)
        rows = h.shape[0]
        h1[a, 0:rows] = before(h).astype(BF)
        h1[a, rows : 2 * rows] = h.astype(BF)
        h1[a, 2 * rows : 3 * rows] = after(h).astype(BF)

    k2 = h1.shape[1]
    for a in range(4):
        valid = ((first_angle + a + 2) >= 0) & ((first_angle + a + 2) < angles)
        h = jnp.dot(w2_ref[...], h1[a : a + 3].reshape(3 * k2, nb), preferred_element_type=F32)
        h2[a] = jnp.where(valid, jnp.maximum(h, 0.0), 0.0).astype(BF)
        parts[a] = jnp.dot(w3_ref[...], h2[a], preferred_element_type=F32)

    nd[...] = jnp.zeros(nd.shape, F32)
    for a in range(2):
        acc = []
        for db in range(3):
            acc.append(sum(parts[a + da, (da * 3 + db) * 16 : (da * 3 + db) * 16 + 16] for da in range(3)))
        result = before(acc[0]) + acc[1] + after(acc[2])
        result = (ds_ref[a].astype(F32) + result[:10]).astype(BF)
        out_ref[a] = result
        lead = result.astype(F32)[:2]
        lead = jnp.concatenate([lead] * 4, axis=0)
        for b in range(blocks):
            nd[a, b] = lead[:, b * 128 : (b + 1) * 128]

    sub = lax.broadcasted_iota(jnp.int32, (8, 128), 0) >> 1

    def cut(g, _):
        full = jnp.zeros((8, 128), F32)
        for i in range(4):
            got = []
            for a in range(2):
                off = off_ref[g * 4 + i, HALO + a]
                q = off >> 7
                r = off & 127
                v = jnp.where(lane >= r, nd[a, q], nd[a, q + 1])
                got.append(pltpu.roll(v, (64 * a + 128 - r) & 127, 1))
            full = jnp.where(sub == i, jnp.where(lane < 64, got[0], got[1]), full)
        pc[pl.ds(pl.multiple_of(g * 8, 8), 8), :] = full
        return 0

    lax.fori_loop(0, tiles // 4, cut, 0)
    piece_ref[...] = pc[...].astype(BF)


def back_kernel(scale, r_ref, u_ref, out_ref):
    j = lax.broadcasted_iota(jnp.int32, (BINS, TX * NY), 0).astype(F32)
    total = jnp.zeros((8, TX * NY), F32)
    zeros = jnp.zeros((6, 128), F32)
    for i in range(r_ref.shape[0] // 4):
        r = r_ref[4 * i : 4 * i + 4, :].astype(F32)
        left = jnp.concatenate(
            [jnp.concatenate([r[0:2], zeros], axis=0), jnp.concatenate([r[2:4], zeros], axis=0)], axis=1
        ).astype(BF)
        right = jnp.concatenate(
            [jnp.maximum(0.0, 1.0 - jnp.abs(u_ref[4 * i + a : 4 * i + a + 1, :] - j)).astype(BF) for a in range(4)],
            axis=0,
        )
        total = total + jnp.dot(left, right, preferred_element_type=F32)
    out_ref[...] = total[0:2] * scale


def call(kernel, outs, scratch, args, smem, mib=24):
    vm = pl.BlockSpec(memory_space=pltpu.VMEM)
    sm = pl.BlockSpec(memory_space=pltpu.SMEM)
    return pl.pallas_call(
        kernel,
        out_shape=outs,
        in_specs=[sm] * smem + [vm] * (len(args) - smem),
        out_specs=[vm] * len(outs),
        scratch_shapes=scratch,
        compiler_params=pltpu.CompilerParams(vmem_limit_bytes=mib * 1024 * 1024),
    )(*args)


def body(
    volume, back_proj, dual_state, sinogram, offsets,
    primal_first, primal_second, primal_third, dual_first, dual_second, dual_third,
):
    wide_count = lax.axis_size("wide")
    slab_count = lax.axis_size("slab")
    w = lax.axis_index("wide")
    s = lax.axis_index("slab")
    mem, zl, pix = volume.shape
    nz = zl * slab_count
    own_angles, nb = dual_state.shape[2], dual_state.shape[3]
    angles = own_angles * wide_count
    hid = primal_first.shape[4]
    scal = jnp.stack([w, s]).astype(jnp.int32)

    rows = (mem + 1) * zl
    xp = jnp.concatenate([volume, back_proj.astype(BF)[None]], axis=0).reshape(rows, pix)
    xd = jnp.concatenate([dual_state, sinogram[None]], axis=0).transpose(0, 1, 2, 3)
    xd = xd.reshape(rows, own_angles * nb)
    both = jnp.concatenate([xp, xd], axis=1)
    both = jnp.concatenate([both, swapped(both, 2)], axis=0)
    xp, xd = both[:, :pix], both[:, pix:]
    xd = jnp.concatenate([xd, swapped(xd, 1)], axis=0)
    edge = HALO * NY
    from_low = shifted("wide", 1, xp[:, pix - edge :])
    from_high = shifted("wide", -1, xp[:, :edge])
    xg = jnp.concatenate([from_low, xp, from_high, jnp.zeros((xp.shape[0], 64), BF)], axis=1)
    xg = jnp.concatenate([xg, swapped(xg, 1)], axis=0)

    all_z = jnp.arange(nz, dtype=jnp.int32)
    def z_order(slab):
        slabs = slab ^ jnp.array([0, 2, 1, 3], jnp.int32)
        return (slabs[:, None] * zl + jnp.arange(zl, dtype=jnp.int32)[None]).reshape(nz)

    seen = z_order(s)
    lead_z = z_order(s & 2)
    e = band(all_z, seen)
    e_out = band(seen, all_z)

    def first_known(wt, e):
        t = jnp.einsum("ypzd,dabco->yoabpcz", e.reshape(-1, slab_count, zl, 3), wt)
        return t.reshape(e.shape[0] * hid, 3, 3 * nz * wt.shape[3])

    pw1 = first_known(primal_first, e).reshape(nz * hid, -1)
    third = jnp.pad(primal_third, ((0, 0),) * 4 + ((0, 1),))
    pw3 = jnp.einsum("pyzd,dabco->abpoyzc", e_out.reshape(slab_count, zl, nz, 3), third)
    pw3 = pw3.reshape(9 * nz * (mem + 1), nz * hid)
    one, two = (zl + 4) * hid, (zl + 2) * hid
    (pw2,) = call(
        lambda *refs: primal_weights_kernel(nz, *refs),
        [jax.ShapeDtypeStruct((nz * hid, 9 * nz * hid), BF)], [], (hidden_base(primal_second),), 0,
    )
    own, lead = call(
        lambda *refs: primal_kernel(wide_count * TX, *refs),
        [jax.ShapeDtypeStruct((mem * zl, pix), BF), jax.ShapeDtypeStruct((nz, pix // 2), BF)],
        [
            pltpu.VMEM((9 * xg.shape[0], xg.shape[1]), BF),
            pltpu.VMEM((9 * nz * hid, xg.shape[1]), BF),
        ],
        (scal, xg, pw1, pw2, pw3), 1,
    )

    sent = jnp.broadcast_to(lead[None], (wide_count, nz, pix // 2))
    gv = lax.all_to_all(sent, "wide", split_axis=0, concat_axis=0, tiled=True)
    gv = gv.reshape(wide_count * nz, pix // 2)

    xd, _ = lax.optimization_barrier((xd, lead))
    end = jnp.where((s & 1) == 0, xd[:, nb:], xd[:, :nb])
    xk = jnp.concatenate([from_sides(xd, 1), from_sides(end, 2)], axis=1)
    xk, dual_first, dual_second, dual_third, w, offsets = lax.optimization_barrier(
        (xk, dual_first, dual_second, dual_third, w, offsets)
    )
    (dw2,) = call(
        lambda *refs: dual_weights_kernel(nz, *refs),
        [jax.ShapeDtypeStruct((two, 9 * one), BF)], [], (scal, hidden_base(dual_second)), 1,
    )
    z_one = s * zl - 2 + jnp.arange(zl + 4, dtype=jnp.int32)
    z_two = s * zl - 1 + jnp.arange(zl + 2, dtype=jnp.int32)
    z_own = s * zl + jnp.arange(zl, dtype=jnp.int32)
    def inside_z(z):
        return ((z >= 0) & (z < nz)).astype(BF)[:, None, None]

    e_one = band(z_one, seen) * inside_z(z_one)
    state_sino = jnp.concatenate([dual_first[:, :, :, :mem], dual_first[:, :, :, mem + 1 :]], axis=3)
    dw1a = first_known(state_sino, e_one)
    e_lead = band(z_one, lead_z) * inside_z(z_one)
    dw1b = jnp.einsum("yzd,dabo->yoabz", e_lead, dual_first[:, :, :, mem]).reshape(one, 3, 3 * nz)
    dw1 = jnp.concatenate([dw1a, dw1b, jnp.zeros((one, 3, 8), BF)], axis=2).reshape(one, -1)
    dw3 = jnp.einsum("yzd,dabco->aboyzc", band(z_own, z_two), dual_third).reshape(9, mem * zl, two)
    dw3 = jnp.pad(dw3, ((0, 0), (0, 16 - mem * zl), (0, 0))).reshape(9 * 16, two)
    near_ids = w * own_angles - HALO + jnp.arange(8, dtype=jnp.int32)
    (table8,) = call(
        table_kernel, [jax.ShapeDtypeStruct((8 * BINS, pix), BF)], [], (positions(near_ids, angles, (s & 1) * (pix // 2)),), 0
    )
    off8 = jnp.take(offsets, jnp.clip(near_ids, 0, angles - 1), axis=1)

    blocks = nb // 128
    ds = dual_state.transpose(2, 0, 1, 3).reshape(own_angles, mem * zl, nb)
    gv, xk, off8, table8, dw1, dw2, dw3, ds = lax.optimization_barrier(
        (gv, xk, off8, table8, dw1, dw2, dw3, ds)
    )
    gv = (gv, swapped(gv, 1))
    xk = (xk, swapped(xk, 1))
    nd, pieces = call(
        lambda *refs: dual_kernel(wide_count, angles, *refs),
        [
            jax.ShapeDtypeStruct((own_angles, mem * zl, nb), BF),
            jax.ShapeDtypeStruct((wide_count * zl, 128), BF),
        ],
        [
            pltpu.VMEM((wide_count * nz, 8 * BINS), F32),
            pltpu.VMEM((8, dw1.shape[1] // 3, nb), BF),
            pltpu.VMEM((6, 3 * one, nb), BF),
            pltpu.VMEM((4, two, nb), BF),
            pltpu.VMEM((4, 9 * 16, nb), F32),
            pltpu.VMEM((own_angles, blocks + 1, 8, 128), F32),
            pltpu.VMEM((wide_count * zl, 128), F32),
        ]
        + [pltpu.VMEM((blocks + 1, 8, 128), F32)] * 8,
        (scal, off8, *gv, table8, xd, *xk, dw1, dw2, dw3, ds), 2, mib=32,
    )
    arrived = lax.all_to_all(
        pieces.reshape(wide_count, zl, 128), "wide", split_axis=0, concat_axis=0, tiled=True
    )
    (new_back,) = call(
        lambda *refs: back_kernel(1.0 / math.sqrt(angles), *refs), [jax.ShapeDtypeStruct((zl, pix), F32)],
        [], (arrived.reshape(wide_count * zl, 128), positions(jnp.arange(angles, dtype=jnp.int32), angles)), 0,
    )
    new_dual = nd.reshape(own_angles, mem, zl, nb).transpose(1, 2, 0, 3)
    return (own.reshape(mem, zl, pix), new_dual, new_back)


def solution(mesh):
    in_specs = (
        P(None, "slab", "wide"),
        P("slab", "wide"),
        P(None, "slab", "wide", None),
        P("slab", "wide", None),
    ) + (P(),) * 7
    out_specs = (P(None, "slab", "wide"), P(None, "slab", "wide", None), P("slab", "wide"))
    return jax.shard_map(body, mesh=mesh, in_specs=in_specs, out_specs=out_specs, check_vma=False)
```

```python
import math

import jax
import jax.numpy as jnp
from jax import lax
from jax.experimental import pallas as pl
from jax.experimental.pallas import tpu as pltpu
from jax.sharding import PartitionSpec as P

NY = 32
TX = 16
BINS = NY + 2 * TX
HALO = 3
BF = jnp.bfloat16
F32 = jnp.float32


def shifted(axis, delta, value):
    size = lax.axis_size(axis)
    return lax.ppermute(value, axis, [(i, i + delta) for i in range(size) if 0 <= i + delta < size])


def band(zo, zi):
    d = jnp.arange(3, dtype=jnp.int32)
    return ((zi[None, :, None] - zo[:, None, None] + 1) == d[None, None, :]).astype(BF)


def from_sides(value, distance):
    wide, slab = lax.axis_size("wide"), lax.axis_size("slab")
    pairs = []
    for i in range(wide):
        for j in range(slab):
            to = i - distance if j % 2 else i + distance
            if 0 <= to < wide:
                pairs.append((i * slab + j, to * slab + j))
    return lax.ppermute(value, ("wide", "slab"), pairs)


def swapped(value, mask):
    size = lax.axis_size("slab")
    return lax.ppermute(value, "slab", [(i, i ^ mask) for i in range(size)])


def hidden_base(w):
    c, o = w.shape[3], w.shape[4]
    base = w.transpose(1, 2, 4, 0, 3).reshape(9, o, 3 * c)
    return jnp.pad(base, ((0, 0), (0, 0), (0, 128 - 3 * c)))


def primal_weights_kernel(nz, p_ref, pout_ref):
    o = p_ref.shape[1]
    width = pout_ref.shape[1] // 9
    c = width // nz
    lane = lax.broadcasted_iota(jnp.int32, (1, width), 1)
    for tap in range(9):
        base = p_ref[tap].astype(F32)
        base = jnp.concatenate([base, jnp.zeros((o, width - base.shape[1]), F32)], axis=1)
        for zo in range(nz):
            moved = pltpu.roll(base, (c * (zo - 1)) % width, 1)
            if zo == 0:
                moved = jnp.where(lane < 2 * c, moved, 0.0)
            elif zo == nz - 1:
                moved = jnp.where(lane >= c * (zo - 1), moved, 0.0)
            pout_ref[zo * o : (zo + 1) * o, tap * width : (tap + 1) * width] = moved.astype(BF)


def dual_weights_kernel(nz, scal_ref, d_ref, dout_ref):
    o = d_ref.shape[1]
    c = dout_ref.shape[1] // 9 // (dout_ref.shape[0] // o + 2)
    width = 256
    count = dout_ref.shape[0] // o
    span = (count + 2) * c
    first = scal_ref[1] * 2 - 1
    for zo in range(count):
        inside = (first + zo >= 0) & (first + zo < nz)
        pieces = []
        for tap in range(9):
            base = d_ref[tap].astype(F32)
            base = jnp.concatenate([base, jnp.zeros((o, width - base.shape[1]), F32)], axis=1)
            pieces.append(pltpu.roll(base, c * zo, 1)[:, :span])
        row = jnp.where(inside, jnp.concatenate(pieces, axis=1), 0.0)
        dout_ref[zo * o : (zo + 1) * o, :] = row.astype(BF)


def table_kernel(u_ref, t_ref):
    j = lax.broadcasted_iota(jnp.int32, (BINS, TX * NY), 0).astype(F32)

    def one(a, _):
        row = u_ref[pl.ds(a, 1), :]
        t_ref[pl.ds(pl.multiple_of(a * BINS, BINS), BINS), :] = jnp.maximum(0.0, 1.0 - jnp.abs(row - j)).astype(BF)
        return 0

    lax.fori_loop(0, u_ref.shape[0], one, 0)


def positions(angle_ids, angle_total, first_pixel=0):
    angle_value = angle_ids.astype(F32) * (math.pi / angle_total)
    pixels = (jnp.arange(TX * NY, dtype=jnp.int32) + first_pixel) % (TX * NY)
    centre_x = (pixels // NY).astype(F32) - (TX - 1) / 2.0
    centre_y = (pixels % NY).astype(F32) - (NY - 1) / 2.0
    return (
        centre_x[None, :] * jnp.cos(angle_value)[:, None]
        + centre_y[None, :] * jnp.sin(angle_value)[:, None]
        + BINS / 2.0
    )


def primal_kernel(nx, scal_ref, x_ref, w1_ref, w2_ref, w3_ref, own_ref, lead_ref, col1, col2):
    lanes = x_ref.shape[1]
    lane = lax.broadcasted_iota(jnp.int32, (1, lanes), 1)
    y = lane & (NY - 1)
    gx = (lane >> 5) - HALO + scal_ref[0] * TX
    inside = (gx >= 0) & (gx < nx)

    def fill(col, value):
        rows = value.shape[0]
        for dx in range(3):
            for dy in range(3):
                shift = NY * (dx - 1) + dy - 1
                moved = value if shift == 0 else pltpu.roll(value, (-shift) % lanes, 1)
                if dy == 0:
                    moved = jnp.where(y == 0, 0.0, moved)
                elif dy == 2:
                    moved = jnp.where(y == NY - 1, 0.0, moved)
                at = (dx * 3 + dy) * rows
                col[at : at + rows, :] = moved.astype(BF)

    x = x_ref[...].astype(F32)
    fill(col1, x)
    h = jnp.dot(w1_ref[...], col1[...], preferred_element_type=F32)
    h = jnp.where(inside, jnp.maximum(h, 0.0), 0.0)
    fill(col2, h)
    h = jnp.dot(w2_ref[...], col2[...], preferred_element_type=F32)
    h = jnp.where(inside, jnp.maximum(h, 0.0), 0.0).astype(BF)
    parts = jnp.dot(w3_ref[...], h, preferred_element_type=F32)
    rows = x.shape[0]
    total = x
    for dy in range(3):
        acc = jnp.zeros((rows, lanes), F32)
        for dx in range(3):
            at = (dx * 3 + dy) * rows
            part = parts[at : at + rows, :]
            if dx != 1:
                part = pltpu.roll(part, (-NY * (dx - 1)) % lanes, 1)
            acc = acc + part
        if dy == 0:
            acc = jnp.where(y == 0, 0.0, pltpu.roll(acc, 1, 1))
        elif dy == 2:
            acc = jnp.where(y == NY - 1, 0.0, pltpu.roll(acc, lanes - 1, 1))
        total = total + acc
    total = pltpu.roll(total, lanes - HALO * NY, 1)[:, : TX * NY]
    per = rows // 4
    lead = jnp.concatenate([total[i * per : i * per + 2] for i in range(4)], axis=0)
    lead = jnp.where((scal_ref[1] & 1) == 0, lead, pltpu.roll(lead, 4, 0))
    half = TX * NY // 2
    lead = jnp.where((scal_ref[1] & 1) == 0, lead[:, :half], lead[:, half:]).astype(BF)
    for tile in range(lead_ref.shape[0]):
        lead_ref[tile] = lead
    own_ref[...] = total[: own_ref.shape[0]].astype(BF)


def before(v):
    bins = lax.broadcasted_iota(jnp.int32, (1, v.shape[1]), 1)
    return jnp.where(bins == 0, 0.0, pltpu.roll(v, 1, 1))


def after(v):
    bins = lax.broadcasted_iota(jnp.int32, (1, v.shape[1]), 1)
    return jnp.where(bins == v.shape[1] - 1, 0.0, pltpu.roll(v, v.shape[1] - 1, 1))


def dual_kernel(tiles, angles, *refs):
    (scal_ref, off_ref, g0_ref, g1_ref, t8_ref, xo_ref, xa_ref, xb_ref, w1_ref, w2_ref, w3_ref, ds_ref, out_ref, piece_ref) = refs[:14]
    (win, x1, h1, h2, parts, nd, pc) = refs[14:21]
    pj = refs[21:]
    nb = x1.shape[2]
    blocks = nb // 128
    lane = lax.broadcasted_iota(jnp.int32, (8, 128), 1)
    first_angle = scal_ref[0] * 2 - HALO

    half = g0_ref.shape[1]
    windows = sum(
        lax.dot_general(ref[...], t8_ref[:, at : at + half], (((1,), (1,)), ((), ())), preferred_element_type=F32)
        for ref, at in ((g0_ref, 0), (g1_ref, half))
    )
    win[...] = windows.astype(BF).astype(F32)
    for ref in pj:
        ref[...] = jnp.zeros(ref.shape, F32)

    def place(t, _):
        found = []
        for a in range(8):
            off = off_ref[t, a]
            q = off >> 7
            r = off & 127
            v = win[pl.ds(pl.multiple_of(t * 8, 8), 8), (a // 2) * 128 : (a // 2) * 128 + 128]
            moved = pltpu.roll(v, (r + 64 * (a % 2)) & 127, 1)
            lo = jnp.where((lane >= r) & (lane < r + 64), moved, 0.0)
            hi = jnp.where(lane < r - 64, moved, 0.0)
            found.append((q, pj[a][q] + lo, pj[a][q + 1] + hi))
        for a, (q, lo, hi) in enumerate(found):
            pj[a][q] = lo
            pj[a][q + 1] = hi
        return 0

    lax.fori_loop(0, tiles, place, 0, unroll=4)

    low_core = (scal_ref[1] & 1) == 0
    for a in range(8):
        valid = ((first_angle + a) >= 0) & ((first_angle + a) < angles)
        proj = jnp.concatenate([pj[a][b] for b in range(blocks)], axis=1) * (1.0 / math.sqrt(NY))
        proj = jnp.where(valid, proj, 0.0).astype(BF).astype(F32)
        if a in (3, 4):
            known = xo_ref[:, (a - 3) * nb : (a - 2) * nb].astype(F32)
        else:
            at = {0: 2, 1: 0, 2: 1, 5: 0, 6: 1, 7: 2}[a] * nb
            mine = xa_ref[:, at : at + nb].astype(F32)
            theirs = xb_ref[:, at : at + nb].astype(F32)
            theirs = jnp.concatenate([theirs[theirs.shape[0] // 2 :], theirs[: theirs.shape[0] // 2]], axis=0)
            known = jnp.where(low_core, mine, theirs) if a < 3 else jnp.where(low_core, theirs, mine)
        x1[a] = jnp.concatenate(
            [before(known), known, after(known), before(proj), proj, after(proj), jnp.zeros((8, nb), F32)], axis=0
        ).astype(BF)

    k1 = x1.shape[1]
    for a in range(6):
        valid = ((first_angle + a + 1) >= 0) & ((first_angle + a + 1) < angles)
        h = jnp.dot(w1_ref[...], x1[a : a + 3].reshape(3 * k1, nb), preferred_element_type=F32)
        h = jnp.where(valid, jnp.maximum(h, 0.0), 0.0)
        rows = h.shape[0]
        h1[a, 0:rows] = before(h).astype(BF)
        h1[a, rows : 2 * rows] = h.astype(BF)
        h1[a, 2 * rows : 3 * rows] = after(h).astype(BF)

    k2 = h1.shape[1]
    for a in range(4):
        valid = ((first_angle + a + 2) >= 0) & ((first_angle + a + 2) < angles)
        h = jnp.dot(w2_ref[...], h1[a : a + 3].reshape(3 * k2, nb), preferred_element_type=F32)
        h2[a] = jnp.where(valid, jnp.maximum(h, 0.0), 0.0).astype(BF)
        parts[a] = jnp.dot(w3_ref[...], h2[a], preferred_element_type=F32)

    nd[...] = jnp.zeros(nd.shape, F32)
    for a in range(2):
        acc = []
        for db in range(3):
            acc.append(sum(parts[a + da, (da * 3 + db) * 16 : (da * 3 + db) * 16 + 16] for da in range(3)))
        result = before(acc[0]) + acc[1] + after(acc[2])
        result = (ds_ref[a].astype(F32) + result[:10]).astype(BF)
        out_ref[a] = result
        lead = result.astype(F32)[:2]
        lead = jnp.concatenate([lead] * 4, axis=0)
        for b in range(blocks):
            nd[a, b] = lead[:, b * 128 : (b + 1) * 128]

    sub = lax.broadcasted_iota(jnp.int32, (8, 128), 0) >> 1

    def cut(g, _):
        full = jnp.zeros((8, 128), F32)
        for i in range(4):
            got = []
            for a in range(2):
                off = off_ref[g * 4 + i, HALO + a]
                q = off >> 7
                r = off & 127
                v = jnp.where(lane >= r, nd[a, q], nd[a, q + 1])
                got.append(pltpu.roll(v, (64 * a + 128 - r) & 127, 1))
            full = jnp.where(sub == i, jnp.where(lane < 64, got[0], got[1]), full)
        pc[pl.ds(pl.multiple_of(g * 8, 8), 8), :] = full
        return 0

    lax.fori_loop(0, tiles // 4, cut, 0, unroll=4)
    piece_ref[...] = pc[...].astype(BF)


def back_kernel(scale, r_ref, u_ref, out_ref):
    j = lax.broadcasted_iota(jnp.int32, (BINS, TX * NY), 0).astype(F32)
    total = jnp.zeros((8, TX * NY), F32)
    zeros = jnp.zeros((6, 128), F32)
    for i in range(r_ref.shape[0] // 4):
        r = r_ref[4 * i : 4 * i + 4, :].astype(F32)
        left = jnp.concatenate(
            [jnp.concatenate([r[0:2], zeros], axis=0), jnp.concatenate([r[2:4], zeros], axis=0)], axis=1
        ).astype(BF)
        right = jnp.concatenate(
            [jnp.maximum(0.0, 1.0 - jnp.abs(u_ref[4 * i + a : 4 * i + a + 1, :] - j)).astype(BF) for a in range(4)],
            axis=0,
        )
        total = total + jnp.dot(left, right, preferred_element_type=F32)
    out_ref[...] = total[0:2] * scale


def call(kernel, outs, scratch, args, smem, mib=24):
    vm = pl.BlockSpec(memory_space=pltpu.VMEM)
    sm = pl.BlockSpec(memory_space=pltpu.SMEM)
    return pl.pallas_call(
        kernel,
        out_shape=outs,
        in_specs=[sm] * smem + [vm] * (len(args) - smem),
        out_specs=[vm] * len(outs),
        scratch_shapes=scratch,
        compiler_params=pltpu.CompilerParams(vmem_limit_bytes=mib * 1024 * 1024),
    )(*args)


def body(
    volume, back_proj, dual_state, sinogram, offsets,
    primal_first, primal_second, primal_third, dual_first, dual_second, dual_third,
):
    wide_count = lax.axis_size("wide")
    slab_count = lax.axis_size("slab")
    w = lax.axis_index("wide")
    s = lax.axis_index("slab")
    mem, zl, pix = volume.shape
    nz = zl * slab_count
    own_angles, nb = dual_state.shape[2], dual_state.shape[3]
    angles = own_angles * wide_count
    hid = primal_first.shape[4]
    scal = jnp.stack([w, s]).astype(jnp.int32)

    rows = (mem + 1) * zl
    xp = jnp.concatenate([volume, back_proj.astype(BF)[None]], axis=0).reshape(rows, pix)
    xd = jnp.concatenate([dual_state, sinogram[None]], axis=0).transpose(0, 1, 2, 3)
    xd = xd.reshape(rows, own_angles * nb)
    both = jnp.concatenate([xp, xd], axis=1)
    both = jnp.concatenate([both, swapped(both, 2)], axis=0)
    xp, xd = both[:, :pix], both[:, pix:]
    xd = jnp.concatenate([xd, swapped(xd, 1)], axis=0)
    edge = HALO * NY
    from_low = shifted("wide", 1, xp[:, pix - edge :])
    from_high = shifted("wide", -1, xp[:, :edge])
    xg = jnp.concatenate([from_low, xp, from_high, jnp.zeros((xp.shape[0], 64), BF)], axis=1)
    xg = jnp.concatenate([xg, swapped(xg, 1)], axis=0)

    all_z = jnp.arange(nz, dtype=jnp.int32)
    def z_order(slab):
        slabs = slab ^ jnp.array([0, 2, 1, 3], jnp.int32)
        return (slabs[:, None] * zl + jnp.arange(zl, dtype=jnp.int32)[None]).reshape(nz)

    seen = z_order(s)
    lead_z = z_order(s & 2)
    e = band(all_z, seen)
    e_out = band(seen, all_z)

    def first_known(wt, e):
        t = jnp.einsum("ypzd,dabco->yoabpcz", e.reshape(-1, slab_count, zl, 3), wt)
        return t.reshape(e.shape[0] * hid, 3, 3 * nz * wt.shape[3])

    pw1 = first_known(primal_first, e).reshape(nz * hid, -1)
    third = jnp.pad(primal_third, ((0, 0),) * 4 + ((0, 1),))
    pw3 = jnp.einsum("pyzd,dabco->abpoyzc", e_out.reshape(slab_count, zl, nz, 3), third)
    pw3 = pw3.reshape(9 * nz * (mem + 1), nz * hid)
    one, two = (zl + 4) * hid, (zl + 2) * hid
    (pw2,) = call(
        lambda *refs: primal_weights_kernel(nz, *refs),
        [jax.ShapeDtypeStruct((nz * hid, 9 * nz * hid), BF)], [], (hidden_base(primal_second),), 0,
    )
    own, lead = call(
        lambda *refs: primal_kernel(wide_count * TX, *refs),
        [jax.ShapeDtypeStruct((mem * zl, pix), BF), jax.ShapeDtypeStruct((wide_count, nz, pix // 2), BF)],
        [
            pltpu.VMEM((9 * xg.shape[0], xg.shape[1]), BF),
            pltpu.VMEM((9 * nz * hid, xg.shape[1]), BF),
        ],
        (scal, xg, pw1, pw2, pw3), 1,
    )

    gv = lax.all_to_all(lead, "wide", split_axis=0, concat_axis=0, tiled=True)
    gv = gv.reshape(wide_count * nz, pix // 2)

    xd, _ = lax.optimization_barrier((xd, lead))
    end = jnp.where((s & 1) == 0, xd[:, nb:], xd[:, :nb])
    xk = jnp.concatenate([from_sides(xd, 1), from_sides(end, 2)], axis=1)
    xk, dual_first, dual_second, dual_third, w, offsets = lax.optimization_barrier(
        (xk, dual_first, dual_second, dual_third, w, offsets)
    )
    (dw2,) = call(
        lambda *refs: dual_weights_kernel(nz, *refs),
        [jax.ShapeDtypeStruct((two, 9 * one), BF)], [], (scal, hidden_base(dual_second)), 1,
    )
    z_one = s * zl - 2 + jnp.arange(zl + 4, dtype=jnp.int32)
    z_two = s * zl - 1 + jnp.arange(zl + 2, dtype=jnp.int32)
    z_own = s * zl + jnp.arange(zl, dtype=jnp.int32)
    def inside_z(z):
        return ((z >= 0) & (z < nz)).astype(BF)[:, None, None]

    e_one = band(z_one, seen) * inside_z(z_one)
    state_sino = jnp.concatenate([dual_first[:, :, :, :mem], dual_first[:, :, :, mem + 1 :]], axis=3)
    dw1a = first_known(state_sino, e_one)
    e_lead = band(z_one, lead_z) * inside_z(z_one)
    dw1b = jnp.einsum("yzd,dabo->yoabz", e_lead, dual_first[:, :, :, mem]).reshape(one, 3, 3 * nz)
    dw1 = jnp.concatenate([dw1a, dw1b, jnp.zeros((one, 3, 8), BF)], axis=2).reshape(one, -1)
    dw3 = jnp.einsum("yzd,dabco->aboyzc", band(z_own, z_two), dual_third).reshape(9, mem * zl, two)
    dw3 = jnp.pad(dw3, ((0, 0), (0, 16 - mem * zl), (0, 0))).reshape(9 * 16, two)
    near_ids = w * own_angles - HALO + jnp.arange(8, dtype=jnp.int32)
    (table8,) = call(
        table_kernel, [jax.ShapeDtypeStruct((8 * BINS, pix), BF)], [], (positions(near_ids, angles, (s & 1) * (pix // 2)),), 0
    )
    off8 = jnp.take(offsets, jnp.clip(near_ids, 0, angles - 1), axis=1)

    blocks = nb // 128
    ds = dual_state.transpose(2, 0, 1, 3).reshape(own_angles, mem * zl, nb)
    gv, xk, off8, table8, dw1, dw2, dw3, ds = lax.optimization_barrier(
        (gv, xk, off8, table8, dw1, dw2, dw3, ds)
    )
    gv = (gv, swapped(gv, 1))
    xk = (xk, swapped(xk, 1))
    nd, pieces = call(
        lambda *refs: dual_kernel(wide_count, angles, *refs),
        [
            jax.ShapeDtypeStruct((own_angles, mem * zl, nb), BF),
            jax.ShapeDtypeStruct((wide_count * zl, 128), BF),
        ],
        [
            pltpu.VMEM((wide_count * nz, 8 * BINS), F32),
            pltpu.VMEM((8, dw1.shape[1] // 3, nb), BF),
            pltpu.VMEM((6, 3 * one, nb), BF),
            pltpu.VMEM((4, two, nb), BF),
            pltpu.VMEM((4, 9 * 16, nb), F32),
            pltpu.VMEM((own_angles, blocks + 1, 8, 128), F32),
            pltpu.VMEM((wide_count * zl, 128), F32),
        ]
        + [pltpu.VMEM((blocks + 1, 8, 128), F32)] * 8,
        (scal, off8, *gv, table8, xd, *xk, dw1, dw2, dw3, ds), 2, mib=32,
    )
    arrived = lax.all_to_all(
        pieces.reshape(wide_count, zl, 128), "wide", split_axis=0, concat_axis=0, tiled=True
    )
    (new_back,) = call(
        lambda *refs: back_kernel(1.0 / math.sqrt(angles), *refs), [jax.ShapeDtypeStruct((zl, pix), F32)],
        [], (arrived.reshape(wide_count * zl, 128), positions(jnp.arange(angles, dtype=jnp.int32), angles)), 0,
    )
    new_dual = nd.reshape(own_angles, mem, zl, nb).transpose(1, 2, 0, 3)
    return (own.reshape(mem, zl, pix), new_dual, new_back)


def solution(mesh):
    in_specs = (
        P(None, "slab", "wide"),
        P("slab", "wide"),
        P(None, "slab", "wide", None),
        P("slab", "wide", None),
    ) + (P(),) * 7
    out_specs = (P(None, "slab", "wide"), P(None, "slab", "wide", None), P("slab", "wide"))
    return jax.shard_map(body, mesh=mesh, in_specs=in_specs, out_specs=out_specs, check_vma=False)
```

```python
import math

import jax
import jax.numpy as jnp
from jax import lax
from jax.experimental import pallas as pl
from jax.experimental.pallas import tpu as pltpu
from jax.sharding import PartitionSpec as P

NY = 32
TX = 16
BINS = NY + 2 * TX
HALO = 3
BF = jnp.bfloat16
F32 = jnp.float32


def shifted(axis, delta, value):
    size = lax.axis_size(axis)
    return lax.ppermute(value, axis, [(i, i + delta) for i in range(size) if 0 <= i + delta < size])


def band(zo, zi):
    d = jnp.arange(3, dtype=jnp.int32)
    return ((zi[None, :, None] - zo[:, None, None] + 1) == d[None, None, :]).astype(BF)


def from_sides(value, distance):
    wide, slab = lax.axis_size("wide"), lax.axis_size("slab")
    pairs = []
    for i in range(wide):
        for j in range(slab):
            to = i - distance if j % 2 else i + distance
            if 0 <= to < wide:
                pairs.append((i * slab + j, to * slab + j))
    return lax.ppermute(value, ("wide", "slab"), pairs)


def swapped(value, mask):
    size = lax.axis_size("slab")
    return lax.ppermute(value, "slab", [(i, i ^ mask) for i in range(size)])


def hidden_base(w):
    c, o = w.shape[3], w.shape[4]
    base = w.transpose(1, 2, 4, 0, 3).reshape(9, o, 3 * c)
    return jnp.pad(base, ((0, 0), (0, 0), (0, 128 - 3 * c)))


def primal_weights_kernel(nz, p_ref, pout_ref):
    o = p_ref.shape[1]
    width = pout_ref.shape[1] // 9
    c = width // nz
    lane = lax.broadcasted_iota(jnp.int32, (1, width), 1)
    for tap in range(9):
        base = p_ref[tap].astype(F32)
        base = jnp.concatenate([base, jnp.zeros((o, width - base.shape[1]), F32)], axis=1)
        for zo in range(nz):
            moved = pltpu.roll(base, (c * (zo - 1)) % width, 1)
            if zo == 0:
                moved = jnp.where(lane < 2 * c, moved, 0.0)
            elif zo == nz - 1:
                moved = jnp.where(lane >= c * (zo - 1), moved, 0.0)
            pout_ref[zo * o : (zo + 1) * o, tap * width : (tap + 1) * width] = moved.astype(BF)


def dual_weights_kernel(nz, scal_ref, d_ref, dout_ref):
    o = d_ref.shape[1]
    c = dout_ref.shape[1] // 9 // (dout_ref.shape[0] // o + 2)
    width = 256
    count = dout_ref.shape[0] // o
    span = (count + 2) * c
    first = scal_ref[1] * 2 - 1
    for zo in range(count):
        inside = (first + zo >= 0) & (first + zo < nz)
        pieces = []
        for tap in range(9):
            base = d_ref[tap].astype(F32)
            base = jnp.concatenate([base, jnp.zeros((o, width - base.shape[1]), F32)], axis=1)
            pieces.append(pltpu.roll(base, c * zo, 1)[:, :span])
        row = jnp.where(inside, jnp.concatenate(pieces, axis=1), 0.0)
        dout_ref[zo * o : (zo + 1) * o, :] = row.astype(BF)


def table_kernel(u_ref, t_ref):
    j = lax.broadcasted_iota(jnp.int32, (BINS, TX * NY), 0).astype(F32)

    def one(a, _):
        row = u_ref[pl.ds(a, 1), :]
        t_ref[pl.ds(pl.multiple_of(a * BINS, BINS), BINS), :] = jnp.maximum(0.0, 1.0 - jnp.abs(row - j)).astype(BF)
        return 0

    lax.fori_loop(0, u_ref.shape[0], one, 0)


def positions(angle_ids, angle_total, first_pixel=0):
    angle_value = angle_ids.astype(F32) * (math.pi / angle_total)
    pixels = (jnp.arange(TX * NY, dtype=jnp.int32) + first_pixel) % (TX * NY)
    centre_x = (pixels // NY).astype(F32) - (TX - 1) / 2.0
    centre_y = (pixels % NY).astype(F32) - (NY - 1) / 2.0
    return (
        centre_x[None, :] * jnp.cos(angle_value)[:, None]
        + centre_y[None, :] * jnp.sin(angle_value)[:, None]
        + BINS / 2.0
    )


def primal_kernel(nx, scal_ref, x_ref, w1_ref, w2_ref, w3_ref, own_ref, lead_ref, col1, col2):
    lanes = x_ref.shape[1]
    lane = lax.broadcasted_iota(jnp.int32, (1, lanes), 1)
    y = lane & (NY - 1)
    gx = (lane >> 5) - HALO + scal_ref[0] * TX
    inside = (gx >= 0) & (gx < nx)

    def fill(col, value):
        rows = value.shape[0]
        for dx in range(3):
            for dy in range(3):
                shift = NY * (dx - 1) + dy - 1
                moved = value if shift == 0 else pltpu.roll(value, (-shift) % lanes, 1)
                if dy == 0:
                    moved = jnp.where(y == 0, 0.0, moved)
                elif dy == 2:
                    moved = jnp.where(y == NY - 1, 0.0, moved)
                at = (dx * 3 + dy) * rows
                col[at : at + rows, :] = moved.astype(BF)

    x = x_ref[...].astype(F32)
    fill(col1, x)
    h = jnp.dot(w1_ref[...], col1[...], preferred_element_type=F32)
    h = jnp.where(inside, jnp.maximum(h, 0.0), 0.0)
    fill(col2, h)
    h = jnp.dot(w2_ref[...], col2[...], preferred_element_type=F32)
    h = jnp.where(inside, jnp.maximum(h, 0.0), 0.0).astype(BF)
    parts = jnp.dot(w3_ref[...], h, preferred_element_type=F32)
    rows = x.shape[0]
    total = x
    for dy in range(3):
        acc = jnp.zeros((rows, lanes), F32)
        for dx in range(3):
            at = (dx * 3 + dy) * rows
            part = parts[at : at + rows, :]
            if dx != 1:
                part = pltpu.roll(part, (-NY * (dx - 1)) % lanes, 1)
            acc = acc + part
        if dy == 0:
            acc = jnp.where(y == 0, 0.0, pltpu.roll(acc, 1, 1))
        elif dy == 2:
            acc = jnp.where(y == NY - 1, 0.0, pltpu.roll(acc, lanes - 1, 1))
        total = total + acc
    total = pltpu.roll(total, lanes - HALO * NY, 1)[:, : TX * NY]
    per = rows // 4
    lead = jnp.concatenate([total[i * per : i * per + 2] for i in range(4)], axis=0)
    lead = jnp.where((scal_ref[1] & 1) == 0, lead, pltpu.roll(lead, 4, 0))
    half = TX * NY // 2
    lead = jnp.where((scal_ref[1] & 1) == 0, lead[:, :half], lead[:, half:]).astype(BF)
    for tile in range(lead_ref.shape[0]):
        lead_ref[tile] = lead
    own_ref[...] = total[: own_ref.shape[0]].astype(BF)


def before(v):
    bins = lax.broadcasted_iota(jnp.int32, (1, v.shape[1]), 1)
    return jnp.where(bins == 0, 0.0, pltpu.roll(v, 1, 1))


def after(v):
    bins = lax.broadcasted_iota(jnp.int32, (1, v.shape[1]), 1)
    return jnp.where(bins == v.shape[1] - 1, 0.0, pltpu.roll(v, v.shape[1] - 1, 1))


def dual_kernel(tiles, angles, *refs):
    (scal_ref, off_ref, g0_ref, g1_ref, t8_ref, xo_ref, xa_ref, xb_ref, w1_ref, w2_ref, w3_ref, ds_ref, out_ref, piece_ref) = refs[:14]
    (win, x1, h1, h2, parts, nd, pc) = refs[14:21]
    pj = refs[21:]
    nb = x1.shape[2]
    blocks = nb // 128
    lane = lax.broadcasted_iota(jnp.int32, (8, 128), 1)
    first_angle = scal_ref[0] * 2 - HALO

    half = g0_ref.shape[1]
    windows = sum(
        lax.dot_general(ref[...], t8_ref[:, at : at + half], (((1,), (1,)), ((), ())), preferred_element_type=F32)
        for ref, at in ((g0_ref, 0), (g1_ref, half))
    )
    win[...] = windows.astype(BF).astype(F32)
    for ref in pj:
        ref[...] = jnp.zeros(ref.shape, F32)

    def place(t, _):
        found = []
        for a in range(8):
            off = off_ref[t, a]
            q = off >> 7
            r = off & 127
            v = win[pl.ds(pl.multiple_of(t * 8, 8), 8), (a // 2) * 128 : (a // 2) * 128 + 128]
            moved = pltpu.roll(v, (r + 64 * (a % 2)) & 127, 1)
            lo = jnp.where((lane >= r) & (lane < r + 64), moved, 0.0)
            hi = jnp.where(lane < r - 64, moved, 0.0)
            found.append((q, pj[a][q] + lo, pj[a][q + 1] + hi))
        for a, (q, lo, hi) in enumerate(found):
            pj[a][q] = lo
            pj[a][q + 1] = hi
        return 0

    lax.fori_loop(0, tiles, place, 0, unroll=8)

    low_core = (scal_ref[1] & 1) == 0
    for a in range(8):
        valid = ((first_angle + a) >= 0) & ((first_angle + a) < angles)
        proj = jnp.concatenate([pj[a][b] for b in range(blocks)], axis=1) * (1.0 / math.sqrt(NY))
        proj = jnp.where(valid, proj, 0.0).astype(BF).astype(F32)
        if a in (3, 4):
            known = xo_ref[:, (a - 3) * nb : (a - 2) * nb].astype(F32)
        else:
            at = {0: 2, 1: 0, 2: 1, 5: 0, 6: 1, 7: 2}[a] * nb
            mine = xa_ref[:, at : at + nb].astype(F32)
            theirs = xb_ref[:, at : at + nb].astype(F32)
            theirs = jnp.concatenate([theirs[theirs.shape[0] // 2 :], theirs[: theirs.shape[0] // 2]], axis=0)
            known = jnp.where(low_core, mine, theirs) if a < 3 else jnp.where(low_core, theirs, mine)
        x1[a] = jnp.concatenate(
            [before(known), known, after(known), before(proj), proj, after(proj), jnp.zeros((8, nb), F32)], axis=0
        ).astype(BF)

    k1 = x1.shape[1]
    for a in range(6):
        valid = ((first_angle + a + 1) >= 0) & ((first_angle + a + 1) < angles)
        h = jnp.dot(w1_ref[...], x1[a : a + 3].reshape(3 * k1, nb), preferred_element_type=F32)
        h = jnp.where(valid, jnp.maximum(h, 0.0), 0.0)
        rows = h.shape[0]
        h1[a, 0:rows] = before(h).astype(BF)
        h1[a, rows : 2 * rows] = h.astype(BF)
        h1[a, 2 * rows : 3 * rows] = after(h).astype(BF)

    k2 = h1.shape[1]
    for a in range(4):
        valid = ((first_angle + a + 2) >= 0) & ((first_angle + a + 2) < angles)
        h = jnp.dot(w2_ref[...], h1[a : a + 3].reshape(3 * k2, nb), preferred_element_type=F32)
        h2[a] = jnp.where(valid, jnp.maximum(h, 0.0), 0.0).astype(BF)
        parts[a] = jnp.dot(w3_ref[...], h2[a], preferred_element_type=F32)

    nd[...] = jnp.zeros(nd.shape, F32)
    for a in range(2):
        acc = []
        for db in range(3):
            acc.append(sum(parts[a + da, (da * 3 + db) * 16 : (da * 3 + db) * 16 + 16] for da in range(3)))
        result = before(acc[0]) + acc[1] + after(acc[2])
        result = (ds_ref[a].astype(F32) + result[:10]).astype(BF)
        out_ref[a] = result
        lead = result.astype(F32)[:2]
        lead = jnp.concatenate([lead] * 4, axis=0)
        for b in range(blocks):
            nd[a, b] = lead[:, b * 128 : (b + 1) * 128]

    sub = lax.broadcasted_iota(jnp.int32, (8, 128), 0) >> 1

    def cut(g, _):
        full = jnp.zeros((8, 128), F32)
        for i in range(4):
            got = []
            for a in range(2):
                off = off_ref[g * 4 + i, HALO + a]
                q = off >> 7
                r = off & 127
                v = jnp.where(lane >= r, nd[a, q], nd[a, q + 1])
                got.append(pltpu.roll(v, (64 * a + 128 - r) & 127, 1))
            full = jnp.where(sub == i, jnp.where(lane < 64, got[0], got[1]), full)
        pc[pl.ds(pl.multiple_of(g * 8, 8), 8), :] = full
        return 0

    lax.fori_loop(0, tiles // 4, cut, 0, unroll=8)
    piece_ref[...] = pc[...].astype(BF)


def back_kernel(scale, r_ref, u_ref, out_ref):
    j = lax.broadcasted_iota(jnp.int32, (BINS, TX * NY), 0).astype(F32)
    total = jnp.zeros((8, TX * NY), F32)
    zeros = jnp.zeros((6, 128), F32)
    for i in range(r_ref.shape[0] // 4):
        r = r_ref[4 * i : 4 * i + 4, :].astype(F32)
        left = jnp.concatenate(
            [jnp.concatenate([r[0:2], zeros], axis=0), jnp.concatenate([r[2:4], zeros], axis=0)], axis=1
        ).astype(BF)
        right = jnp.concatenate(
            [jnp.maximum(0.0, 1.0 - jnp.abs(u_ref[4 * i + a : 4 * i + a + 1, :] - j)).astype(BF) for a in range(4)],
            axis=0,
        )
        total = total + jnp.dot(left, right, preferred_element_type=F32)
    out_ref[...] = total[0:2] * scale


def call(kernel, outs, scratch, args, smem, mib=24):
    vm = pl.BlockSpec(memory_space=pltpu.VMEM)
    sm = pl.BlockSpec(memory_space=pltpu.SMEM)
    return pl.pallas_call(
        kernel,
        out_shape=outs,
        in_specs=[sm] * smem + [vm] * (len(args) - smem),
        out_specs=[vm] * len(outs),
        scratch_shapes=scratch,
        compiler_params=pltpu.CompilerParams(vmem_limit_bytes=mib * 1024 * 1024),
    )(*args)


def body(
    volume, back_proj, dual_state, sinogram, offsets,
    primal_first, primal_second, primal_third, dual_first, dual_second, dual_third,
):
    wide_count = lax.axis_size("wide")
    slab_count = lax.axis_size("slab")
    w = lax.axis_index("wide")
    s = lax.axis_index("slab")
    mem, zl, pix = volume.shape
    nz = zl * slab_count
    own_angles, nb = dual_state.shape[2], dual_state.shape[3]
    angles = own_angles * wide_count
    hid = primal_first.shape[4]
    scal = jnp.stack([w, s]).astype(jnp.int32)

    rows = (mem + 1) * zl
    xp = jnp.concatenate([volume, back_proj.astype(BF)[None]], axis=0).reshape(rows, pix)
    xd = jnp.concatenate([dual_state, sinogram[None]], axis=0).transpose(0, 1, 2, 3)
    xd = xd.reshape(rows, own_angles * nb)
    both = jnp.concatenate([xp, xd], axis=1)
    both = jnp.concatenate([both, swapped(both, 2)], axis=0)
    xp, xd = both[:, :pix], both[:, pix:]
    xd = jnp.concatenate([xd, swapped(xd, 1)], axis=0)
    edge = HALO * NY
    from_low = shifted("wide", 1, xp[:, pix - edge :])
    from_high = shifted("wide", -1, xp[:, :edge])
    xg = jnp.concatenate([from_low, xp, from_high, jnp.zeros((xp.shape[0], 64), BF)], axis=1)
    xg = jnp.concatenate([xg, swapped(xg, 1)], axis=0)

    all_z = jnp.arange(nz, dtype=jnp.int32)
    def z_order(slab):
        slabs = slab ^ jnp.array([0, 2, 1, 3], jnp.int32)
        return (slabs[:, None] * zl + jnp.arange(zl, dtype=jnp.int32)[None]).reshape(nz)

    seen = z_order(s)
    lead_z = z_order(s & 2)
    e = band(all_z, seen)
    e_out = band(seen, all_z)

    def first_known(wt, e):
        t = jnp.einsum("ypzd,dabco->yoabpcz", e.reshape(-1, slab_count, zl, 3), wt)
        return t.reshape(e.shape[0] * hid, 3, 3 * nz * wt.shape[3])

    pw1 = first_known(primal_first, e).reshape(nz * hid, -1)
    third = jnp.pad(primal_third, ((0, 0),) * 4 + ((0, 1),))
    pw3 = jnp.einsum("pyzd,dabco->abpoyzc", e_out.reshape(slab_count, zl, nz, 3), third)
    pw3 = pw3.reshape(9 * nz * (mem + 1), nz * hid)
    one, two = (zl + 4) * hid, (zl + 2) * hid
    (pw2,) = call(
        lambda *refs: primal_weights_kernel(nz, *refs),
        [jax.ShapeDtypeStruct((nz * hid, 9 * nz * hid), BF)], [], (hidden_base(primal_second),), 0,
    )
    own, lead = call(
        lambda *refs: primal_kernel(wide_count * TX, *refs),
        [jax.ShapeDtypeStruct((mem * zl, pix), BF), jax.ShapeDtypeStruct((wide_count, nz, pix // 2), BF)],
        [
            pltpu.VMEM((9 * xg.shape[0], xg.shape[1]), BF),
            pltpu.VMEM((9 * nz * hid, xg.shape[1]), BF),
        ],
        (scal, xg, pw1, pw2, pw3), 1,
    )

    gv = lax.all_to_all(lead, "wide", split_axis=0, concat_axis=0, tiled=True)
    gv = gv.reshape(wide_count * nz, pix // 2)

    xd, _ = lax.optimization_barrier((xd, lead))
    end = jnp.where((s & 1) == 0, xd[:, nb:], xd[:, :nb])
    xk = jnp.concatenate([from_sides(xd, 1), from_sides(end, 2)], axis=1)
    xk, dual_first, dual_second, dual_third, w, offsets = lax.optimization_barrier(
        (xk, dual_first, dual_second, dual_third, w, offsets)
    )
    (dw2,) = call(
        lambda *refs: dual_weights_kernel(nz, *refs),
        [jax.ShapeDtypeStruct((two, 9 * one), BF)], [], (scal, hidden_base(dual_second)), 1,
    )
    z_one = s * zl - 2 + jnp.arange(zl + 4, dtype=jnp.int32)
    z_two = s * zl - 1 + jnp.arange(zl + 2, dtype=jnp.int32)
    z_own = s * zl + jnp.arange(zl, dtype=jnp.int32)
    def inside_z(z):
        return ((z >= 0) & (z < nz)).astype(BF)[:, None, None]

    e_one = band(z_one, seen) * inside_z(z_one)
    state_sino = jnp.concatenate([dual_first[:, :, :, :mem], dual_first[:, :, :, mem + 1 :]], axis=3)
    dw1a = first_known(state_sino, e_one)
    e_lead = band(z_one, lead_z) * inside_z(z_one)
    dw1b = jnp.einsum("yzd,dabo->yoabz", e_lead, dual_first[:, :, :, mem]).reshape(one, 3, 3 * nz)
    dw1 = jnp.concatenate([dw1a, dw1b, jnp.zeros((one, 3, 8), BF)], axis=2).reshape(one, -1)
    dw3 = jnp.einsum("yzd,dabco->aboyzc", band(z_own, z_two), dual_third).reshape(9, mem * zl, two)
    dw3 = jnp.pad(dw3, ((0, 0), (0, 16 - mem * zl), (0, 0))).reshape(9 * 16, two)
    near_ids = w * own_angles - HALO + jnp.arange(8, dtype=jnp.int32)
    (table8,) = call(
        table_kernel, [jax.ShapeDtypeStruct((8 * BINS, pix), BF)], [], (positions(near_ids, angles, (s & 1) * (pix // 2)),), 0
    )
    off8 = jnp.take(offsets, jnp.clip(near_ids, 0, angles - 1), axis=1)

    blocks = nb // 128
    ds = dual_state.transpose(2, 0, 1, 3).reshape(own_angles, mem * zl, nb)
    gv, xk, off8, table8, dw1, dw2, dw3, ds = lax.optimization_barrier(
        (gv, xk, off8, table8, dw1, dw2, dw3, ds)
    )
    gv = (gv, swapped(gv, 1))
    xk = (xk, swapped(xk, 1))
    nd, pieces = call(
        lambda *refs: dual_kernel(wide_count, angles, *refs),
        [
            jax.ShapeDtypeStruct((own_angles, mem * zl, nb), BF),
            jax.ShapeDtypeStruct((wide_count * zl, 128), BF),
        ],
        [
            pltpu.VMEM((wide_count * nz, 8 * BINS), F32),
            pltpu.VMEM((8, dw1.shape[1] // 3, nb), BF),
            pltpu.VMEM((6, 3 * one, nb), BF),
            pltpu.VMEM((4, two, nb), BF),
            pltpu.VMEM((4, 9 * 16, nb), F32),
            pltpu.VMEM((own_angles, blocks + 1, 8, 128), F32),
            pltpu.VMEM((wide_count * zl, 128), F32),
        ]
        + [pltpu.VMEM((blocks + 1, 8, 128), F32)] * 8,
        (scal, off8, *gv, table8, xd, *xk, dw1, dw2, dw3, ds), 2, mib=32,
    )
    arrived = lax.all_to_all(
        pieces.reshape(wide_count, zl, 128), "wide", split_axis=0, concat_axis=0, tiled=True
    )
    (new_back,) = call(
        lambda *refs: back_kernel(1.0 / math.sqrt(angles), *refs), [jax.ShapeDtypeStruct((zl, pix), F32)],
        [], (arrived.reshape(wide_count * zl, 128), positions(jnp.arange(angles, dtype=jnp.int32), angles)), 0,
    )
    new_dual = nd.reshape(own_angles, mem, zl, nb).transpose(1, 2, 0, 3)
    return (own.reshape(mem, zl, pix), new_dual, new_back)


def solution(mesh):
    in_specs = (
        P(None, "slab", "wide"),
        P("slab", "wide"),
        P(None, "slab", "wide", None),
        P("slab", "wide", None),
    ) + (P(),) * 7
    out_specs = (P(None, "slab", "wide"), P(None, "slab", "wide", None), P("slab", "wide"))
    return jax.shard_map(body, mesh=mesh, in_specs=in_specs, out_specs=out_specs, check_vma=False)
```
